256 devices in a mesh: row: 16 (over y, x), col: 8 (over z), feat: 2 (over core).
Axes of the slice: x: 4, y: 4, z: 8, core: 2. Of those that a mesh axis runs over, the one named last changes fastest.
Arguments:
- tiles: bfloat16 [16, 8, 128, 128, 128], P('row', 'col'), may hold values from -0.0625 to 0.0625
- coords: int32 [16, 8, 128, 2], P('row', 'col'), may hold values from 0 to 15, as said below
- counts: int32 [16, 8], P('row', 'col'), may hold values from 16 to 128, as said below
- features: bfloat16 [16384, 1024], P(('col', 'row')), may hold values from -24 to 24
- weight: bfloat16 [1024, 1024], P(None, 'feat'), may hold values from -0.1875 to 0.1875
- grad_out: bfloat16 [32768, 1024], P('row', 'feat'), may hold values from -6 to 6
Outputs:
- layer_out: bfloat16 [32768, 1024], P('row', 'feat')
- weight_grad: float32 [1024, 1024], P(('row', 'col'), 'feat')
- input_grad: bfloat16 [16384, 1024], P(('col', 'row'), 'feat')
The draws below stay inside these ranges and needn't reach their ends.
Inputs may be any that keep to these rules, and one draw needn't show every extreme that they name: `coords`: column 0 is a tile row below 16, column 1 a tile column below 16; the slots of one block name distinct tiles. Slots 0 to counts - 1 of a block are live, the others are to be ignored.
All inputs are finite; a program needn't handle non-finite values.
Results may differ from the reference program's by a relative error of at most 0.017.
Values may be sent and summed in bfloat16 or wider, within the bound.
A program may use at most 128 MiB of HBM per device.

```python
import jax
import jax.numpy as jnp
from jax import lax

F = 1024
H = 1024
TILE = 128
ROW_TILES = 16
COL_TILES = 16
TILES = 128
NROWS = 32768
NCOLS = 16384
N_ROW = 16
N_COL = 8


def tile_lists(key):
    blocks = N_ROW * N_COL
    cells = ROW_TILES * COL_TILES
    positions = jnp.arange(cells, dtype=jnp.int32)
    scores = jax.random.randint(jax.random.fold_in(key, 11), (blocks, cells), 0, 1 << 20)
    scores = scores * cells + positions[None, :]
    chosen = jax.random.randint(jax.random.fold_in(key, 12), (), 0, blocks)
    block_ids = jnp.arange(blocks, dtype=jnp.int32)
    forced = jnp.where(positions == 0, -2, jnp.where(positions == cells - 1, -1, 0))
    on_chosen = (block_ids == chosen)[:, None] & (forced[None, :] < 0)
    scores = jnp.where(on_chosen, forced[None, :], scores)
    order = jnp.argsort(scores, axis=1, stable=True)[:, :TILES].astype(jnp.int32)
    coords = jnp.stack([order // COL_TILES, order % COL_TILES], axis=-1)
    coords = coords.reshape(N_ROW, N_COL, TILES, 2)
    lowest = max(1, TILES // 8)
    spread = jax.random.randint(jax.random.fold_in(key, 13), (blocks,), 0, 1024)
    counts = lowest + (TILES - lowest) * spread * spread // (1023 * 1023)
    offset = jax.random.randint(jax.random.fold_in(key, 14), (), 0, blocks - 1)
    other = (chosen + 1 + offset) % blocks
    counts = jnp.where(block_ids == chosen, TILES, jnp.where(block_ids == other, lowest, counts))
    return (coords, counts.reshape(N_ROW, N_COL).astype(jnp.int32))


def draw_coords(key, part):
    coords, counts = tile_lists(key)
    return coords


def draw_counts(key, part):
    coords, counts = tile_lists(key)
    return counts


def raised(values, own_key, source, target, parts, factor):
    def block_of(axis_at):
        return (jnp.arange(values.shape[axis_at]) // (values.shape[axis_at] // parts)).reshape((-1,) + (1,) * (values.ndim - 1 - axis_at))

    near = jax.random.permutation(own_key, parts)[block_of(target)]
    far = (block_of(target) + parts // 2) % parts
    return jnp.where((block_of(source) == near) | (block_of(source) == far), factor * values, values)


def steps_of(stream_key, dims, pieces, least, largest):
    def one(axis_at, parts):
        heights = jax.random.uniform(jax.random.fold_in(jax.random.fold_in(stream_key, 6), axis_at), (parts,), jnp.float32, least / len(pieces), largest / len(pieces))
        return jnp.repeat(jnp.exp(heights), dims[axis_at] // parts).reshape((-1,) + (1,) * (len(dims) - axis_at - 1))

    factor_of = one(*pieces[0])
    for cut in pieces[1:]:
        factor_of = factor_of * one(*cut)
    return factor_of


def normal_values(stream_key, dims, scale, limit, shards=(), held_as=jnp.bfloat16):
    drawn = jax.random.normal(stream_key, dims, jnp.float32) * scale
    if len(shards) > 0:
        drawn = steps_of(stream_key, dims, shards, -0.22, 0.18) * drawn
    return jnp.clip(drawn, min=-limit, max=limit).astype(held_as)


def noise_with(rng, shape, scale, bound, cuts, heavy, held_as=jnp.bfloat16):
    values = scale * jax.random.normal(rng, shape, jnp.float32)
    if cuts:
        values = values * steps_of(rng, shape, cuts, -0.22, 0.18)
    return jnp.clip(raised(values, jax.random.fold_in(rng, 3), *heavy), -bound, bound).astype(held_as)


def setup_inputs(seed: int = 0) -> dict:
    key_of = jax.random.split(jax.random.key(seed), 7)
    return {
        "tiles": normal_values(key_of[0], (N_ROW, N_COL, TILES, TILE, TILE), (TILES * N_COL * TILE // ROW_TILES) ** -0.5, 0.0625, ((0, 16), (1, 8))),
        "coords": draw_coords(jax.random.fold_in(key_of[6], 71), 0),
        "counts": draw_counts(jax.random.fold_in(key_of[6], 71), 0),
        "features": noise_with(key_of[3], (NCOLS, F), 1.0, 24.0, ((0, 128),), (0, 1, 128, 5.5)),
        "weight": normal_values(key_of[4], (F, H), F ** -0.5, 0.1875, ((1, 2),)),
        "grad_out": normal_values(key_of[5], (NROWS, H), 1.0, 6.0, ((0, 16), (1, 2))),
    }


def silu_slope(value):
    sig = jax.nn.sigmoid(value)
    return sig * (1.0 + value * (1.0 - sig))


def reference(tiles, coords, counts, features, weight, grad_out):
    projected = jnp.dot(features, weight, preferred_element_type=jnp.float32).astype(jnp.bfloat16)
    hidden = weight.shape[1]
    dense = projected.reshape(N_COL, COL_TILES, TILE, hidden)
    slot_index = jnp.arange(TILES, dtype=jnp.int32)
    tile_rows = jnp.arange(ROW_TILES, dtype=jnp.int32)
    tile_cols = jnp.arange(COL_TILES, dtype=jnp.int32)

    def forward_block(total, inputs):
        block_tiles, block_coords, block_count, block_dense = inputs
        live = (slot_index < block_count).astype(jnp.float32)
        picked = block_dense[block_coords[:, 1]].astype(jnp.float32)
        prod = jnp.einsum("kij,kjh->kih", block_tiles.astype(jnp.float32), picked)
        onehot = (block_coords[:, 0][None, :] == tile_rows[:, None]).astype(jnp.float32) * live[None, :]
        return total + jnp.einsum("rk,kih->rih", onehot, prod), None

    def forward_row(inputs):
        row_tiles, row_coords, row_counts = inputs
        start = jnp.zeros((ROW_TILES, TILE, hidden), jnp.float32)
        total, unused = lax.scan(forward_block, start, (row_tiles, row_coords, row_counts, dense))
        return total

    pre = lax.map(forward_row, (tiles, coords, counts)).reshape(NROWS, hidden)
    layer_out = jax.nn.silu(pre).astype(jnp.bfloat16)
    delta = (grad_out.astype(jnp.float32) * silu_slope(pre)).astype(jnp.bfloat16)
    delta_rows = delta.reshape(N_ROW, ROW_TILES, TILE, hidden)

    def backward_row(total, inputs):
        row_tiles, row_coords, row_counts, row_delta = inputs

        def backward_block(item):
            block_tiles, block_coords, block_count = item
            live = (slot_index < block_count).astype(jnp.float32)
            picked = row_delta[block_coords[:, 0]].astype(jnp.float32)
            prod = jnp.einsum("kji,kjh->kih", block_tiles.astype(jnp.float32), picked)
            onehot = (block_coords[:, 1][None, :] == tile_cols[:, None]).astype(jnp.float32) * live[None, :]
            return jnp.einsum("ck,kih->cih", onehot, prod)

        terms = lax.map(backward_block, (row_tiles, row_coords, row_counts))
        return total + terms, None

    start = jnp.zeros((N_COL, COL_TILES, TILE, hidden), jnp.float32)
    back_sum, unused = lax.scan(backward_row, start, (tiles, coords, counts, delta_rows))
    back = back_sum.reshape(NCOLS, hidden).astype(jnp.bfloat16)
    weight_grad = jnp.dot(features.T, back, preferred_element_type=jnp.float32) * (NCOLS ** -0.5)
    input_grad = jnp.dot(back, weight.T, preferred_element_type=jnp.float32).astype(jnp.bfloat16)
    return layer_out, weight_grad, input_grad
```

```python
import jax
import jax.numpy as jnp
from jax import lax
from jax.sharding import PartitionSpec as P

BF16 = jnp.bfloat16
F32 = jnp.float32


def silu_slope(value):
    sig = jax.nn.sigmoid(value)
    return sig * (1.0 + value * (1.0 - sig))


def densify(tiles, coords, count, row_tiles, col_tiles):
    slots, edge = tiles.shape[0], tiles.shape[1]
    place = coords[:, 0] * col_tiles + coords[:, 1]
    slot = jnp.arange(slots, dtype=jnp.int32)
    cell = jnp.arange(row_tiles * col_tiles, dtype=jnp.int32)
    hit = (place[None, :] == cell[:, None]) & (slot[None, :] < count)
    where_from = jnp.sum(jnp.where(hit, slot[None, :], 0), axis=1)
    live = jnp.any(hit, axis=1)
    picked = jnp.where(live[:, None, None], tiles[where_from], jnp.zeros((), tiles.dtype))
    dense = picked.reshape(row_tiles, col_tiles, edge, edge).transpose(0, 2, 1, 3)
    return dense.reshape(row_tiles * edge, col_tiles * edge)


def on_device(tiles, coords, counts, features, weight, grad_out):
    edge = tiles.shape[-1]
    row_tiles = grad_out.shape[0] // edge
    col_tiles = features.shape[0] * lax.axis_size("row") // edge
    dense = densify(tiles[0, 0], coords[0, 0], counts[0, 0], row_tiles, col_tiles)
    projected = jnp.dot(features, weight, preferred_element_type=F32).astype(BF16)
    column_block = lax.all_gather(projected, "row", axis=0, tiled=True)
    partial_value = jnp.dot(dense, column_block, preferred_element_type=F32).astype(BF16)
    own = lax.psum_scatter(partial_value, "col", scatter_dimension=0, tiled=True)
    pre = lax.all_gather(own, "col", axis=0, tiled=True).astype(F32)
    layer_out = jax.nn.silu(pre).astype(BF16)
    delta = (grad_out.astype(F32) * silu_slope(pre)).astype(BF16)
    back_partial = lax.dot_general(
        dense, delta, (((0,), (0,)), ((), ())), preferred_element_type=F32
    ).astype(BF16)
    back = lax.psum_scatter(back_partial, "row", scatter_dimension=0, tiled=True)
    node_total = features.shape[0] * lax.axis_size("row") * lax.axis_size("col")
    scale = node_total ** (-0.5)
    product = lax.dot_general(
        features, back, (((0,), (0,)), ((), ())), preferred_element_type=F32
    )
    summed = lax.psum_scatter((product * scale).astype(BF16), "row", scatter_dimension=0, tiled=True)
    weight_grad = lax.psum_scatter(summed, "col", scatter_dimension=0, tiled=True).astype(F32)
    input_terms = lax.dot_general(
        back, weight, (((1,), (1,)), ((), ())), preferred_element_type=F32
    ).astype(BF16)
    input_grad = lax.psum_scatter(input_terms, "feat", scatter_dimension=1, tiled=True)
    return (layer_out, weight_grad, input_grad)


def solution(mesh):
    return jax.shard_map(
        on_device,
        mesh=mesh,
        in_specs=(
            P("row", "col", None, None, None),
            P("row", "col", None, None),
            P("row", "col"),
            P(("col", "row"), None),
            P(None, "feat"),
            P("row", "feat"),
        ),
        out_specs=(P("row", "feat"), P(("row", "col"), "feat"), P(("col", "row"), "feat")),
        check_vma=False,
    )
```

```python
import functools

import jax
import jax.numpy as jnp
from jax import lax
from jax.experimental import pallas as pl
from jax.experimental.pallas import tpu as pltpu
from jax.sharding import PartitionSpec as P

BF16 = jnp.bfloat16
F32 = jnp.float32
MESH = pl.DeviceIdType.MESH
VMEM = pltpu.VMEM

SIDE = 4
DEPTH = 8
TILE = 128
ROWS = 2048
SLAB = ROWS // DEPTH
HALF = SLAB // 2
WIDE = 512
INNER = 1024
CHUNKS = 2
HC = WIDE // CHUNKS
STAGGER = 2

DN_T = (((0,), (0,)), ((), ()))
DN_N = (((1,), (1,)), ((), ()))


def f32dot(a, b, dims=(((1,), (0,)), ((), ()))):
    return lax.dot_general(a, b, dims, preferred_element_type=F32)


def kernel(
    slot_of, tiles_hbm, feat_hbm, weight_hbm, gout_hbm,
    layer_hbm, wgrad, igrad,
    tiles, adj, feat, weight, gout, layer,
    gath, part, zsend_p, zsend_m, zrecv_p, zrecv_m, pre, delta, bpart, back,
    wpart, wown, wz, terms, terms_send, terms_recv,
    bs1, bs2, bs3, bs4, br1, br2, br3, br4, bown,
    ws1, ws2, ws3, ws4, wr1, wr2, wr3, wr4, wsum,
    local_sem, out_sem, send_sem, recv_sem,
):
    row = lax.axis_index("row")
    z = lax.axis_index("col")
    f = lax.axis_index("feat")
    y, x = row // SIDE, row % SIDE

    def at(dy, dx, dz):
        return (((y + dy + SIDE) % SIDE) * SIDE + (x + dx + SIDE) % SIDE, (z + dz + DEPTH) % DEPTH, f)

    xp, xm = at(0, 1, 0), at(0, -1, 0)
    yp, ym = at(1, 0, 0), at(-1, 0, 0)
    zpeer = [None] + [at(0, 0, d) for d in range(1, DEPTH)]
    zp, zm = zpeer[1], zpeer[DEPTH - 1]
    other = (row, z, 1 - f)

    loads = [
        pltpu.make_async_copy(weight_hbm, weight, local_sem.at[0]),
        pltpu.make_async_copy(feat_hbm, feat, local_sem.at[1]),
        pltpu.make_async_copy(tiles_hbm, tiles.at[0:TILE], local_sem.at[2]),
        pltpu.make_async_copy(gout_hbm, gout, local_sem.at[3]),
    ]
    for load in loads:
        load.start()

    barrier = pltpu.get_barrier_semaphore()
    partners = [xp, xm, yp, ym, other] + zpeer[1:]
    for device in partners:
        pl.semaphore_signal(barrier, inc=1, device_id=device, device_id_type=MESH)

    sent = []

    def send(src, dst, to):
        n = len(sent)
        copy = pltpu.make_async_remote_copy(
            src_ref=src, dst_ref=dst, send_sem=send_sem.at[n], recv_sem=recv_sem.at[n],
            device_id=to, device_id_type=MESH,
        )
        copy.start()
        sent.append(copy)
        return copy

    def arrive(copies):
        for copy in copies:
            copy.wait_recv()

    def lay_out(first, count):
        def one(n, carry):
            slab = first + n // 2
            tile_row = ((z + slab) % DEPTH) * 2 + n % 2
            start = pl.multiple_of((slab * 2 + n % 2) * TILE, TILE)
            for i in range(SIDE):
                for j in range(SIDE):
                    tile_col = ((y + i) % SIDE) * SIDE + (x + j) % SIDE
                    slot = slot_of[tile_row * SIDE * SIDE + tile_col]
                    c = (i * SIDE + j) * TILE
                    adj[pl.ds(start, TILE), c : c + TILE] = tiles[slot]
            return carry

        lax.fori_loop(0, 2 * count, one, 0)

    def scatter_sum(first, last, acc, s1, s2, s3, s4, r1, r2, r3, r4, own, q):
        for t in range(SIDE):
            s1[0, t] = acc(2, t, 0, q).astype(BF16)
            s1[1, t] = acc(2, t, q, 2 * q).astype(BF16)
        c1 = [send(s1.at[d], r1.at[d], first[d]) for d in range(2)]
        yield
        arrive(c1)
        for t in range(SIDE):
            s2[0, t, 0:q] = (acc(1, t, 0, q) + r1[0, t].astype(F32)).astype(BF16)
            s2[0, t, q : 2 * q] = acc(1, t, q, 2 * q).astype(BF16)
            s2[1, t, 0:q] = acc(3, t, 0, q).astype(BF16)
            s2[1, t, q : 2 * q] = (acc(3, t, q, 2 * q) + r1[1, t].astype(F32)).astype(BF16)
        c2 = [send(s2.at[d], r2.at[d], first[d]) for d in range(2)]
        yield
        arrive(c2)
        for t in (2, 1, 3, 0):
            own[t] = acc(0, t, 0, 2 * q) + r2[0, t].astype(F32) + r2[1, t].astype(F32)
            if t == 2:
                s3[0] = own[2, 0:q].astype(BF16)
                s3[1] = own[2, q : 2 * q].astype(BF16)
                c3 = [send(s3.at[d], r3.at[d], last[d]) for d in range(2)]
        yield
        arrive(c3)
        s4[0, 0:q] = (own[1, 0:q] + r3[0].astype(F32)).astype(BF16)
        s4[0, q : 2 * q] = own[1, q : 2 * q].astype(BF16)
        s4[1, 0:q] = own[3, 0:q].astype(BF16)
        s4[1, q : 2 * q] = (own[3, q : 2 * q] + r3[1].astype(F32)).astype(BF16)
        c4 = [send(s4.at[d], r4.at[d], last[d]) for d in range(2)]
        yield
        arrive(c4)
        return own[0] + r4[0].astype(F32) + r4[1].astype(F32)

    def together(flows):
        results = [None] * len(flows)
        live = list(range(len(flows)))
        while live:
            for n in list(live):
                try:
                    next(flows[n])
                except StopIteration as stop:
                    results[n] = stop.value
                    live.remove(n)
            if live:
                yield
        return results

    def activate(k, i):
        start = pl.multiple_of(((z + i) % DEPTH) * SLAB, SLAB)
        cols = slice(k * HC, (k + 1) * HC)
        value = pre[k, i].astype(F32)
        sig = 1.0 / (1.0 + jnp.exp(-value))
        layer[pl.ds(start, SLAB), cols] = (value * sig).astype(BF16)
        slope = sig * (1.0 + value * (1.0 - sig))
        delta[k, i * SLAB : (i + 1) * SLAB] = (gout[pl.ds(start, SLAB), cols].astype(F32) * slope).astype(BF16)

    def flow(k):
        cols = slice(k * HC, (k + 1) * HC)
        if k == 0:
            loads[0].wait()
            loads[1].wait()
            for n in range(CHUNKS):
                gath[n, 0, 0] = f32dot(feat[...], weight[:, n * HC : (n + 1) * HC]).astype(BF16)
            pl.semaphore_wait(barrier, len(partners))
        g = gath.at[k]
        h, q = TILE // 2, TILE // 4
        c = [
            send(g.at[0, 0, 0:h], g.at[0, 3, 0:h], xp),
            send(g.at[0, 0, 0:h], g.at[0, 1, 0:h], xm),
            send(g.at[0, 0, h:TILE], g.at[3, 0, h:TILE], yp),
            send(g.at[0, 0, h:TILE], g.at[1, 0, h:TILE], ym),
        ]
        if k == 0:
            loads[2].wait()
            tiles[TILE] = jnp.zeros((TILE, TILE), BF16)
            lay_out(3, 3)
        yield
        arrive(c)
        c = [
            send(g.at[0, 3, 0:q], g.at[0, 2, 0:q], xp),
            send(g.at[0, 1, q:h], g.at[0, 2, q:h], xm),
            send(g.at[3, 0, h : h + q], g.at[2, 0, h : h + q], yp),
            send(g.at[1, 0, h + q : TILE], g.at[2, 0, h + q : TILE], ym),
        ]
        if k == 0:
            lay_out(0, 3)
            lay_out(6, 2)
        yield
        arrive(c)
        c = [
            send(g.at[0, :, 0:h], g.at[3, :, 0:h], yp),
            send(g.at[0, :, 0:h], g.at[1, :, 0:h], ym),
            send(g.at[:, 0, h:TILE], g.at[:, 3, h:TILE], xp),
            send(g.at[:, 0, h:TILE], g.at[:, 1, h:TILE], xm),
        ]
        yield
        arrive(c)
        c = [
            send(g.at[3, :, 0:q], g.at[2, :, 0:q], yp),
            send(g.at[1, :, q:h], g.at[2, :, q:h], ym),
            send(g.at[:, 3, h : h + q], g.at[:, 2, h : h + q], xp),
            send(g.at[:, 1, h + q : TILE], g.at[:, 2, h + q : TILE], xm),
        ]
        yield
        arrive(c)

        def slabs(first, last):
            block = gath[k].reshape(ROWS, HC)
            value = f32dot(adj[first * SLAB : last * SLAB, :], block)
            part[k, first:last] = value.reshape(last - first, SLAB, HC)

        top, low = slice(0, HALF), slice(HALF, SLAB)
        slabs(3, 6)
        zsend_p[k, 0, top] = part[k, 4, top].astype(BF16)
        zsend_p[k, 0, low] = part[k, 3, low].astype(BF16)
        zsend_m[k, 0, top] = part[k, 5, top].astype(BF16)
        zsend_m[k, 0, low] = part[k, 4, low].astype(BF16)
        c = [
            send(zsend_p.at[k, 0], zrecv_p.at[k, 0], zp),
            send(zsend_m.at[k, 0], zrecv_m.at[k, 0], zm),
        ]
        slabs(6, 8)
        slabs(0, 3)
        yield
        for s in (1, 2):
            arrive(c)
            rp, rm = zrecv_p.at[k, s - 1], zrecv_m.at[k, s - 1]
            zsend_p[k, s, top] = (part[k, 4 - s, top] + rp[top].astype(F32)).astype(BF16)
            zsend_p[k, s, low] = (part[k, 3 - s, low] + rp[low].astype(F32)).astype(BF16)
            zsend_m[k, s, top] = (part[k, 5 + s, top] + rm[top].astype(F32)).astype(BF16)
            zsend_m[k, s, low] = (part[k, 4 + s, low] + rm[low].astype(F32)).astype(BF16)
            c = [
                send(zsend_p.at[k, s], zrecv_p.at[k, s], zp),
                send(zsend_m.at[k, s], zrecv_m.at[k, s], zm),
            ]
            yield
        arrive(c)
        zsend_p[k, 3, top] = (part[k, 1, top] + zrecv_p[k, 2, top].astype(F32)).astype(BF16)
        zsend_m[k, 3, low] = (part[k, 7, low] + zrecv_m[k, 2, low].astype(F32)).astype(BF16)
        c = [
            send(zsend_p.at[k, 3, top], zrecv_p.at[k, 3, top], zp),
            send(zsend_m.at[k, 3, low], zrecv_m.at[k, 3, low], zm),
        ]
        yield
        arrive(c)
        pre[k, 0, top] = (part[k, 0, top] + zrecv_m[k, 2, top].astype(F32) + zrecv_p[k, 3, top].astype(F32)).astype(BF16)
        pre[k, 0, low] = (part[k, 0, low] + zrecv_p[k, 2, low].astype(F32) + zrecv_m[k, 3, low].astype(F32)).astype(BF16)

        c = [send(pre.at[k, 0], pre.at[k, 7], zp), send(pre.at[k, 0], pre.at[k, 1], zm)]
        if k == 0:
            loads[3].wait()
        activate(k, 0)
        yield
        for s in (1, 2):
            arrive(c)
            c = [
                send(pre.at[k, 8 - s], pre.at[k, 7 - s], zp),
                send(pre.at[k, s], pre.at[k, s + 1], zm),
            ]
            activate(k, 8 - s)
            activate(k, s)
            yield
        arrive(c)
        c = [
            send(pre.at[k, 5, top], pre.at[k, 4, top], zp),
            send(pre.at[k, 3, low], pre.at[k, 4, low], zm),
        ]
        activate(k, 5)
        activate(k, 3)
        yield
        arrive(c)
        activate(k, 4)
        out = pltpu.make_async_copy(layer.at[:, cols], layer_hbm.at[:, cols], out_sem.at[k])
        out.start()
        outs.append(out)

        def columns(i):
            for n in range(2):
                c0 = i * 4 * TILE + n * 2 * TILE
                bpart[k, c0 : c0 + 2 * TILE] = f32dot(adj[:, c0 : c0 + 2 * TILE], delta[k], DN_T)

        def term(i, j, lo, hi):
            c0 = (i * SIDE + j) * TILE
            return bpart[k, c0 + lo : c0 + hi]

        for i in (2, 1, 3, 0):
            columns(i)
        res = yield from together([
            scatter_sum((yp, ym), (xp, xm), lambda a, t, lo, hi: term(a, t, lo, hi),
                        bs1.at[k, 0], bs2.at[k, 0], bs3.at[k, 0], bs4.at[k, 0],
                        br1.at[k, 0], br2.at[k, 0], br3.at[k, 0], br4.at[k, 0], bown.at[k, 0], q),
            scatter_sum((xp, xm), (yp, ym), lambda a, t, lo, hi: term(t, a, h + lo, h + hi),
                        bs1.at[k, 1], bs2.at[k, 1], bs3.at[k, 1], bs4.at[k, 1],
                        br1.at[k, 1], br2.at[k, 1], br3.at[k, 1], br4.at[k, 1], bown.at[k, 1], q),
        ])
        back[k, 0:h] = res[0].astype(BF16)
        back[k, h:TILE] = res[1].astype(BF16)

        wpart[k] = f32dot(feat[...], back[k], DN_T) * ((ROWS * DEPTH) ** -0.5)

        def wterm(i, j, lo, hi):
            start = (((y + i) % SIDE) * SIDE + (x + j) % SIDE) * (INNER // 16) + lo
            return wpart[k, pl.ds(pl.multiple_of(start, 16), hi - lo)]

        flows = [
            scatter_sum((yp, ym), (xp, xm), lambda a, t, lo, hi: wterm(a, t, lo, hi),
                        ws1.at[k, 0], ws2.at[k, 0], ws3.at[k, 0], ws4.at[k, 0],
                        wr1.at[k, 0], wr2.at[k, 0], wr3.at[k, 0], wr4.at[k, 0], wsum.at[k, 0], 16),
            scatter_sum((xp, xm), (yp, ym), lambda a, t, lo, hi: wterm(t, a, 32 + lo, 32 + hi),
                        ws1.at[k, 1], ws2.at[k, 1], ws3.at[k, 1], ws4.at[k, 1],
                        wr1.at[k, 1], wr2.at[k, 1], wr3.at[k, 1], wr4.at[k, 1], wsum.at[k, 1], 16),
        ]
        wflow = together(flows)
        next(wflow)

        mine = f32dot(back[k], weight[pl.ds(pl.multiple_of(f * WIDE, WIDE), WIDE), cols], DN_N)
        theirs = f32dot(back[k], weight[pl.ds(pl.multiple_of((1 - f) * WIDE, WIDE), WIDE), cols], DN_N)
        if k == 0:
            terms[0] = mine
            terms[1] = theirs
        else:
            terms[0] += mine
            terms[1] += theirs
        if k == CHUNKS - 1:
            terms_send[...] = terms[1].astype(BF16)
            swap = send(terms_send, terms_recv, other)
        yield
        res = yield from wflow
        wown[k, 0:32] = res[0]
        wown[k, 32:64] = res[1]
        c = []
        for d in range(1, DEPTH):
            start = pl.multiple_of(((z + d) % DEPTH) * 8, 8)
            c.append(send(wown.at[k, pl.ds(start, 8)], wz.at[k, d], zpeer[d]))
        total = wown[k, pl.ds(pl.multiple_of(z * 8, 8), 8)]
        if k == CHUNKS - 1:
            swap.wait_recv()
            igrad[...] = (terms[0] + terms_recv[...].astype(F32)).astype(BF16)
        yield
        arrive(c)
        for d in range(1, DEPTH):
            total = total + wz[k, d]
        wgrad[:, cols] = total

    outs = []
    flows = {k: flow(k) for k in range(CHUNKS)}
    tick = 0
    while flows:
        for k in sorted(flows):
            if tick >= k * STAGGER:
                try:
                    next(flows[k])
                except StopIteration:
                    del flows[k]
        tick += 1
    for out in outs:
        out.wait()
    for copy in sent:
        copy.wait_send()


def slot_table(coords, count):
    place = coords[:, 0] * (SIDE * SIDE) + coords[:, 1]
    slot = jnp.arange(TILE, dtype=jnp.int32)
    cell = jnp.arange(SIDE * SIDE * SIDE * SIDE, dtype=jnp.int32)
    hit = (place[None, :] == cell[:, None]) & (slot[None, :] < count)
    return jnp.min(jnp.where(hit, slot[None, :], TILE), axis=1)


def on_device(tiles, coords, counts, features, weight, grad_out):
    k2 = (CHUNKS, 2)
    q, w = TILE // 4, 16

    def sums(rows):
        return [
            VMEM((CHUNKS, 2, 2, SIDE, rows, HC), BF16),
            VMEM((CHUNKS, 2, 2, SIDE, 2 * rows, HC), BF16),
            VMEM((CHUNKS, 2, 2, rows, HC), BF16),
            VMEM((CHUNKS, 2, 2, 2 * rows, HC), BF16),
        ]

    scratch = [
        VMEM((TILE + 1, TILE, TILE), BF16),
        VMEM((ROWS, ROWS), BF16),
        VMEM((TILE, INNER), BF16),
        VMEM((INNER, WIDE), BF16),
        VMEM((ROWS, WIDE), BF16),
        VMEM((ROWS, WIDE), BF16),
        VMEM((CHUNKS, SIDE, SIDE, TILE, HC), BF16),
        VMEM((CHUNKS, DEPTH, SLAB, HC), F32),
        VMEM((CHUNKS, 4, SLAB, HC), BF16),
        VMEM((CHUNKS, 4, SLAB, HC), BF16),
        VMEM((CHUNKS, 4, SLAB, HC), BF16),
        VMEM((CHUNKS, 4, SLAB, HC), BF16),
        VMEM((CHUNKS, DEPTH, SLAB, HC), BF16),
        VMEM((CHUNKS, ROWS, HC), BF16),
        VMEM((CHUNKS, ROWS, HC), F32),
        VMEM((CHUNKS, TILE, HC), BF16),
        VMEM((CHUNKS, INNER, HC), F32),
        VMEM((CHUNKS, INNER // 16, HC), F32),
        VMEM((CHUNKS, DEPTH, 8, HC), F32),
        VMEM((2, TILE, WIDE), F32),
        VMEM((TILE, WIDE), BF16),
        VMEM((TILE, WIDE), BF16),
        *sums(q), *sums(q), VMEM((CHUNKS, 2, SIDE, 2 * q, HC), F32),
        *sums(w), *sums(w), VMEM((CHUNKS, 2, SIDE, 2 * w, HC), F32),
        pltpu.SemaphoreType.DMA((4,)),
        pltpu.SemaphoreType.DMA((CHUNKS,)),
        pltpu.SemaphoreType.DMA((71 * CHUNKS + 1,)),
        pltpu.SemaphoreType.DMA((71 * CHUNKS + 1,)),
    ]
    anywhere = pl.BlockSpec(memory_space=pl.ANY)
    return pl.pallas_call(
        kernel,
        out_shape=(
            jax.ShapeDtypeStruct((ROWS, WIDE), BF16),
            jax.ShapeDtypeStruct((8, WIDE), F32),
            jax.ShapeDtypeStruct((TILE, WIDE), BF16),
        ),
        in_specs=[pl.BlockSpec(memory_space=pltpu.SMEM)] + [anywhere] * 4,
        out_specs=(anywhere, pl.BlockSpec(memory_space=VMEM), pl.BlockSpec(memory_space=VMEM)),
        scratch_shapes=scratch,
        compiler_params=pltpu.CompilerParams(
            collective_id=0, has_side_effects=True, vmem_limit_bytes=60 * 1024 * 1024
        ),
        cost_estimate=pl.CostEstimate(flops=9 * 10**9, bytes_accessed=10 * 2**20, transcendentals=2 * 2**20),
        name="graph_layer",
    )(slot_table(coords[0, 0], counts[0, 0]), tiles[0, 0], features, weight, grad_out)


def solution(mesh):
    return jax.shard_map(
        on_device,
        mesh=mesh,
        in_specs=(
            P("row", "col", None, None, None),
            P("row", "col", None, None),
            P("row", "col"),
            P(("col", "row"), None),
            P(None, "feat"),
            P("row", "feat"),
        ),
        out_specs=(P("row", "feat"), P(("row", "col"), "feat"), P(("col", "row"), "feat")),
        check_vma=False,
    )
```

```python
import functools

import jax
import jax.numpy as jnp
from jax import lax
from jax.experimental import pallas as pl
from jax.experimental.pallas import tpu as pltpu
from jax.sharding import PartitionSpec as P

BF16 = jnp.bfloat16
F32 = jnp.float32
MESH = pl.DeviceIdType.MESH
VMEM = pltpu.VMEM

VMEM_LIMIT = 60 * 1024 * 1024
SIDE = 4
DEPTH = 8
TILE = 128
ROWS = 2048
SLAB = ROWS // DEPTH
HALF = SLAB // 2
WIDE = 512
INNER = 1024
WIDTHS = (256, 128, 128)
PARTS = len(WIDTHS)
ORDER = (
    0, 9, 1, 0, 1, 0, 1, 2, 0, 1, 2, 9, 0, 2, 1, 0, 2, 9, 1, 2, 0, 9, 2, 0, 1, 0, 1, 9, 2, 0,
    2, 1, 0, 1, 2, 9, 0, 1, 2, 0, 3, 6, 1, 2, 3, 1, 4, 6, 7, 2, 3, 4, 2, 5, 8, 7, 3, 6, 4, 8,
    5, 7, 8, 6, 4, 3, 5, 7, 8, 4, 6, 5, 7, 8, 5, 7, 8, 6, 5,
)
FIRST = [sum(WIDTHS[:k]) for k in range(len(WIDTHS))]
LAST = PARTS - 1
SLOTS = 21

DN_T = (((0,), (0,)), ((), ()))
DN_N = (((1,), (1,)), ((), ()))


def f32dot(a, b, dims=(((1,), (0,)), ((), ()))):
    return lax.dot_general(a, b, dims, preferred_element_type=F32)


def kernel(names, slot_of, tiles_hbm, feat_hbm, weight_hbm, gout_hbm, layer_hbm, wgrad, igrad, *refs):
    r = dict(zip(names, refs))
    tiles, adj, feat, weight, gout, layer = (r[n] for n in ("tiles", "adj", "feat", "weight", "gout", "layer"))
    nodes, terms, terms_send, terms_recv = (r[n] for n in ("nodes", "terms", "terms_send", "terms_recv"))
    local_sem, out_sem, send_sem, recv_sem = (r[n] for n in ("local_sem", "out_sem", "send_sem", "recv_sem"))
    row = lax.axis_index("row")
    z = lax.axis_index("col")
    f = lax.axis_index("feat")
    y, x = row // SIDE, row % SIDE

    def at(dy, dx, dz):
        return (((y + dy + SIDE) % SIDE) * SIDE + (x + dx + SIDE) % SIDE, (z + dz + DEPTH) % DEPTH, f)

    xp, xm = at(0, 1, 0), at(0, -1, 0)
    yp, ym = at(1, 0, 0), at(-1, 0, 0)
    ways = [xp, xm, yp, ym]
    zpeer = [None] + [at(0, 0, d) for d in range(1, DEPTH)]
    zp, zm = zpeer[1], zpeer[DEPTH - 1]
    other = (row, z, 1 - f)

    def weight_load(k):
        cols = slice(FIRST[k], FIRST[k] + WIDTHS[k])
        return pltpu.make_async_copy(weight_hbm.at[:, cols], weight.at[:, cols], local_sem.at[3 + k])

    loads = [
        pltpu.make_async_copy(feat_hbm, feat, local_sem.at[0]),
        weight_load(0),
        pltpu.make_async_copy(tiles_hbm, tiles.at[0:TILE], local_sem.at[1]),
        *[weight_load(k) for k in range(1, LAST + 1)],
        pltpu.make_async_copy(gout_hbm, gout, local_sem.at[2]),
    ]
    for load in loads:
        load.start()

    barrier = pltpu.get_barrier_semaphore()
    partners = [xp, xm, yp, ym, other] + zpeer[1:]
    for device in partners:
        pl.semaphore_signal(barrier, inc=1, device_id=device, device_id_type=MESH)

    def send(src, dst, to, slot):
        copy = pltpu.make_async_remote_copy(
            src_ref=src, dst_ref=dst, send_sem=send_sem.at[slot], recv_sem=recv_sem.at[slot],
            device_id=to, device_id_type=MESH,
        )
        copy.start()
        return copy

    def arrive(copies):
        for copy in copies:
            copy.wait_recv()
        for copy in copies:
            copy.wait_send()

    def lay_out(first, count):
        def one(n, carry):
            slab = first + n // 2
            tile_row = ((z + slab) % DEPTH) * 2 + n % 2
            start = pl.multiple_of((slab * 2 + n % 2) * TILE, TILE)
            for i in range(SIDE):
                for j in range(SIDE):
                    tile_col = ((y + i) % SIDE) * SIDE + (x + j) % SIDE
                    slot = slot_of[tile_row * SIDE * SIDE + tile_col]
                    c = (i * SIDE + j) * TILE
                    adj[pl.ds(start, TILE), c : c + TILE] = tiles[slot]
            return carry

        lax.fori_loop(0, 2 * count, one, 0)

    def scatter_sum(term, bufs, q, slot):
        s1, s2, s3, s4, r1, r2, r3, r4, own = bufs
        first, last = ((2, 3), (0, 1)), ((0, 1), (2, 3))

        def acc(side, a, t, lo, hi):
            return term(a, t, lo, hi) if side == 0 else term(t, a, 2 * q + lo, 2 * q + hi)

        def send_all(src, dst, to, phase):
            return [
                send(src.at[n, d], dst.at[n, d], ways[to[n][d]], slot + 2 * to[n][d] + phase % 2)
                for n in range(2)
                for d in range(2)
            ]

        for n in range(2):
            for t in range(SIDE):
                s1[n, 0, t] = acc(n, 2, t, 0, q).astype(BF16)
                s1[n, 1, t] = acc(n, 2, t, q, 2 * q).astype(BF16)
        c = send_all(s1, r1, first, 0)
        yield
        arrive(c)
        for n in range(2):
            for t in range(SIDE):
                s2[n, 0, t, 0:q] = (acc(n, 1, t, 0, q) + r1[n, 0, t].astype(F32)).astype(BF16)
                s2[n, 0, t, q : 2 * q] = acc(n, 1, t, q, 2 * q).astype(BF16)
                s2[n, 1, t, 0:q] = acc(n, 3, t, 0, q).astype(BF16)
                s2[n, 1, t, q : 2 * q] = (acc(n, 3, t, q, 2 * q) + r1[n, 1, t].astype(F32)).astype(BF16)
        c = send_all(s2, r2, first, 1)
        yield
        arrive(c)

        def add(n, t):
            own[n, t] = acc(n, 0, t, 0, 2 * q) + r2[n, 0, t].astype(F32) + r2[n, 1, t].astype(F32)

        for n in range(2):
            add(n, 2)
            s3[n, 0] = own[n, 2, 0:q].astype(BF16)
            s3[n, 1] = own[n, 2, q : 2 * q].astype(BF16)
        c = send_all(s3, r3, last, 2)
        for n in range(2):
            for t in (1, 3, 0):
                add(n, t)
        yield
        arrive(c)
        for n in range(2):
            s4[n, 0, 0:q] = (own[n, 1, 0:q] + r3[n, 0].astype(F32)).astype(BF16)
            s4[n, 0, q : 2 * q] = own[n, 1, q : 2 * q].astype(BF16)
            s4[n, 1, 0:q] = own[n, 3, 0:q].astype(BF16)
            s4[n, 1, q : 2 * q] = (own[n, 3, q : 2 * q] + r3[n, 1].astype(F32)).astype(BF16)
        c = send_all(s4, r4, last, 3)
        yield
        arrive(c)
        return [own[n, 0] + r4[n, 0].astype(F32) + r4[n, 1].astype(F32) for n in range(2)]

    def plane_gather(g, slot):
        h, q = TILE // 2, TILE // 4

        def send_all(phase, *moves):
            return [
                send(src, dst, to, slot + 2 * n + phase % 2)
                for n, (src, dst, to) in enumerate(zip(moves[0::2], moves[1::2], (xp, xm, yp, ym)))
            ]

        own_h, own_l = g.at[0, 0, 0:h], g.at[0, 0, h:TILE]
        c = send_all(
            0, own_h, g.at[0, 3, 0:h], own_h, g.at[0, 1, 0:h],
            own_l, g.at[3, 0, h:TILE], own_l, g.at[1, 0, h:TILE],
        )
        yield
        arrive(c)
        c = send_all(
            1, g.at[0, 3, 0:q], g.at[0, 2, 0:q], g.at[0, 1, q:h], g.at[0, 2, q:h],
            g.at[3, 0, h : h + q], g.at[2, 0, h : h + q], g.at[1, 0, h + q : TILE], g.at[2, 0, h + q : TILE],
        )
        yield
        arrive(c)
        c = send_all(
            2, g.at[:, 0, h:TILE], g.at[:, 3, h:TILE], g.at[:, 0, h:TILE], g.at[:, 1, h:TILE],
            g.at[0, :, 0:h], g.at[3, :, 0:h], g.at[0, :, 0:h], g.at[1, :, 0:h],
        )
        yield
        arrive(c)
        c = send_all(
            3, g.at[:, 3, h : h + q], g.at[:, 2, h : h + q], g.at[:, 1, h + q : TILE], g.at[:, 2, h + q : TILE],
            g.at[3, :, 0:q], g.at[2, :, 0:q], g.at[1, :, q:h], g.at[2, :, q:h],
        )
        yield
        arrive(c)

    def gather_features():
        mine = nodes.at[f]
        for n in range(2):

            @pl.when(f == n)
            def _():
                nodes[n, 0, 0] = feat[:, n * WIDE : (n + 1) * WIDE]

        yield from plane_gather(mine, SLOTS * PARTS)
        c = [send(mine, nodes.at[f], other, SLOTS * PARTS + 8)]
        yield
        arrive(c)

    def flow(k):
        hc, slot = WIDTHS[k], SLOTS * k
        cols = slice(FIRST[k], FIRST[k] + hc)
        g, part, pre, delta, bsum, bpart = (r[n + str(k)] for n in ("gath", "part", "pre", "delta", "bsum", "bpart"))
        zsend_p, zsend_m, zrecv_p, zrecv_m = (r[n + str(k)] for n in ("zsend_p", "zsend_m", "zrecv_p", "zrecv_m"))

        if k == 0:
            loads[0].wait()
        loads[1 if k == 0 else 2 + k].wait()
        g[0, 0] = f32dot(feat[...], weight[:, cols]).astype(BF16)
        if k == 0:
            pl.semaphore_wait(barrier, len(partners))
        gather = plane_gather(g, slot)
        next(gather)
        if k == 0:
            loads[2].wait()
            tiles[TILE] = jnp.zeros((TILE, TILE), BF16)
            lay_out(3, 3)
        yield
        next(gather)
        if k == 0:
            lay_out(0, 3)
            lay_out(6, 2)
        yield
        yield from gather

        def slabs(first, last):
            value = f32dot(adj[first * SLAB : last * SLAB, :], g[...].reshape(ROWS, hc))
            part[first:last] = value.reshape(last - first, SLAB, hc)

        def send_z(step, up, down):
            return [send(*up, zp, slot + 16 + step % 2), send(*down, zm, slot + 18 + step % 2)]

        top, low = slice(0, HALF), slice(HALF, SLAB)
        slabs(3, 6)
        zsend_p[0, top] = part[4, top].astype(BF16)
        zsend_p[0, low] = part[3, low].astype(BF16)
        zsend_m[0, top] = part[5, top].astype(BF16)
        zsend_m[0, low] = part[4, low].astype(BF16)
        c = send_z(0, (zsend_p.at[0], zrecv_p.at[0]), (zsend_m.at[0], zrecv_m.at[0]))
        slabs(6, 8)
        slabs(0, 3)
        yield
        for s in (1, 2):
            arrive(c)
            zsend_p[s, top] = (part[4 - s, top] + zrecv_p[s - 1, top].astype(F32)).astype(BF16)
            zsend_p[s, low] = (part[3 - s, low] + zrecv_p[s - 1, low].astype(F32)).astype(BF16)
            zsend_m[s, top] = (part[5 + s, top] + zrecv_m[s - 1, top].astype(F32)).astype(BF16)
            zsend_m[s, low] = (part[4 + s, low] + zrecv_m[s - 1, low].astype(F32)).astype(BF16)
            c = send_z(s, (zsend_p.at[s], zrecv_p.at[s]), (zsend_m.at[s], zrecv_m.at[s]))
            yield
        arrive(c)
        zsend_p[3, top] = (part[1, top] + zrecv_p[2, top].astype(F32)).astype(BF16)
        zsend_m[3, low] = (part[7, low] + zrecv_m[2, low].astype(F32)).astype(BF16)
        c = send_z(3, (zsend_p.at[3, top], zrecv_p.at[3, top]), (zsend_m.at[3, low], zrecv_m.at[3, low]))
        yield
        arrive(c)
        pre[0, top] = (part[0, top] + zrecv_m[2, top].astype(F32) + zrecv_p[3, top].astype(F32)).astype(BF16)
        pre[0, low] = (part[0, low] + zrecv_p[2, low].astype(F32) + zrecv_m[3, low].astype(F32)).astype(BF16)

        def activate(i):
            start = pl.multiple_of(((z + i) % DEPTH) * SLAB, SLAB)
            value = pre[i].astype(F32)
            sig = 0.5 + 0.5 * jnp.tanh(0.5 * value)
            layer[pl.ds(start, SLAB), cols] = (value * sig).astype(BF16)
            slope = sig * (1.0 + value * (1.0 - sig))
            delta[i * SLAB : (i + 1) * SLAB] = (gout[pl.ds(start, SLAB), cols].astype(F32) * slope).astype(BF16)

        c = send_z(4, (pre.at[0], pre.at[7]), (pre.at[0], pre.at[1]))
        if k == 0:
            loads[-1].wait()
        activate(0)
        yield
        for s in (1, 2):
            arrive(c)
            c = send_z(4 + s, (pre.at[8 - s], pre.at[7 - s]), (pre.at[s], pre.at[s + 1]))
            activate(8 - s)
            activate(s)
            yield
        arrive(c)
        c = send_z(7, (pre.at[5, top], pre.at[4, top]), (pre.at[3, low], pre.at[4, low]))
        activate(5)
        activate(3)
        for n in range(DEPTH):
            c0 = n * SLAB
            bsum[c0 : c0 + SLAB] = f32dot(adj[0 : 4 * SLAB, c0 : c0 + SLAB], delta[0 : 4 * SLAB], DN_T) + f32dot(
                adj[5 * SLAB :, c0 : c0 + SLAB], delta[5 * SLAB :], DN_T
            )
        yield
        arrive(c)
        activate(4)
        mid = slice(4 * SLAB, 5 * SLAB)
        for n in (4, 5, 0, 1, 2, 3, 6, 7):
            c0 = n * SLAB
            value = bsum[c0 : c0 + SLAB] + f32dot(adj[mid, c0 : c0 + SLAB], delta[mid], DN_T)
            bpart[n // 2, n % 2 * 2 : n % 2 * 2 + 2] = value.astype(BF16).reshape(2, TILE, hc)
        out = pltpu.make_async_copy(layer.at[:, cols], layer_hbm.at[:, cols], out_sem.at[k])
        out.start()
        outs.append(out)

    def sum_back(k):
        hc = WIDTHS[k]
        cols = slice(FIRST[k], FIRST[k] + hc)
        bpart, back = r["bpart" + str(k)], r["back" + str(k)]

        def term(i, j, lo, hi):
            return bpart[i, j, lo:hi].astype(F32)

        res = yield from scatter_sum(term, sum_refs("b", k), TILE // 4, SLOTS * k)
        back[0 : TILE // 2] = res[0].astype(BF16)
        back[TILE // 2 : TILE] = res[1].astype(BF16)
        theirs = f32dot(back[...], weight[pl.ds(pl.multiple_of((1 - f) * WIDE, WIDE), WIDE), cols], DN_N)
        if k > 0:
            theirs += terms[1]
        if k < LAST:
            terms[1] = theirs
        else:
            terms_send[...] = theirs.astype(BF16)
            swap = [send(terms_send, terms_recv, other, SLOTS * PARTS + 9)]
        mine = f32dot(back[...], weight[pl.ds(pl.multiple_of(f * WIDE, WIDE), WIDE), cols], DN_N)
        if k > 0:
            mine += terms[0]
        terms[0] = mine
        if k == LAST:
            yield
            arrive(swap)
            igrad[...] = (terms[0] + terms_recv[...].astype(F32)).astype(BF16)

    def sum_weight(k):
        hc = WIDTHS[k]
        cols = slice(FIRST[k], FIRST[k] + hc)
        bpart, wpart, wown, wz = (r[n + str(k)] for n in ("bpart", "wpart", "wown", "wz"))
        block = bpart[...].reshape(ROWS, hc)
        for n in range(2):
            value = f32dot(nodes[n].reshape(ROWS, WIDE), block, DN_T)
            wpart[n * WIDE : (n + 1) * WIDE] = value * ((ROWS * DEPTH) ** -0.5)

        def term(i, j, lo, hi):
            start = (((y + i) % SIDE) * SIDE + (x + j) % SIDE) * (INNER // 16) + lo
            return wpart[pl.ds(pl.multiple_of(start, 16), hi - lo)]

        res = yield from scatter_sum(term, sum_refs("w", k), 16, SLOTS * k + 8)
        wown[0:32] = res[0]
        wown[32:64] = res[1]
        slot = SLOTS * k + 20
        for d in range(1, DEPTH):
            start = pl.multiple_of(((z + d) % DEPTH) * 8, 8)
            send(wown.at[pl.ds(start, 8)], wz.at[d], zpeer[d], slot)
        yield
        others = wz.at[1:DEPTH]
        pltpu.make_async_copy(others, others, recv_sem.at[slot]).wait()
        pltpu.make_async_copy(others, others, send_sem.at[slot]).wait()
        total = wown[pl.ds(pl.multiple_of(z * 8, 8), 8)]
        for d in range(1, DEPTH):
            total = total + wz[d]
        wgrad[:, cols] = total

    def sum_refs(kind, k):
        return [r[kind + n + str(k)] for n in ("s1", "s2", "s3", "s4", "r1", "r2", "r3", "r4", "acc")]

    outs = []
    flows = [make(k) for make in (flow, sum_back, sum_weight) for k in range(PARTS)] + [gather_features()]
    for n in ORDER:
        next(flows[n], None)
    for out in outs:
        out.wait()


def slot_table(coords, count):
    place = coords[:, 0] * (SIDE * SIDE) + coords[:, 1]
    slot = jnp.arange(TILE, dtype=jnp.int32)
    cell = jnp.arange(SIDE * SIDE * SIDE * SIDE, dtype=jnp.int32)
    hit = (place[None, :] == cell[:, None]) & (slot[None, :] < count)
    return jnp.min(jnp.where(hit, slot[None, :], TILE), axis=1)


def scratch_of():
    dma = pltpu.SemaphoreType.DMA
    slots = SLOTS * PARTS + 10
    refs = {
        "tiles": VMEM((TILE + 1, TILE, TILE), BF16),
        "adj": VMEM((ROWS, ROWS), BF16),
        "feat": VMEM((TILE, INNER), BF16),
        "weight": VMEM((INNER, WIDE), BF16),
        "gout": VMEM((ROWS, WIDE), BF16),
        "layer": VMEM((ROWS, WIDE), BF16),
        "nodes": VMEM((2, SIDE, SIDE, TILE, WIDE), BF16),
        "terms": VMEM((2, TILE, WIDE), F32),
        "terms_send": VMEM((TILE, WIDE), BF16),
        "terms_recv": VMEM((TILE, WIDE), BF16),
        "local_sem": dma((3 + len(WIDTHS),)),
        "out_sem": dma((len(WIDTHS),)),
        "send_sem": dma((slots,)),
        "recv_sem": dma((slots,)),
    }
    for k, hc in enumerate(WIDTHS):
        shapes = {
            "gath": ((SIDE, SIDE, TILE, hc), BF16),
            "part": ((DEPTH, SLAB, hc), F32),
            "zsend_p": ((4, SLAB, hc), BF16),
            "zsend_m": ((4, SLAB, hc), BF16),
            "zrecv_p": ((4, SLAB, hc), BF16),
            "zrecv_m": ((4, SLAB, hc), BF16),
            "pre": ((DEPTH, SLAB, hc), BF16),
            "delta": ((ROWS, hc), BF16),
            "bsum": ((ROWS, hc), F32),
            "bpart": ((SIDE, SIDE, TILE, hc), BF16),
            "back": ((TILE, hc), BF16),
            "wpart": ((INNER, hc), F32),
            "wown": ((INNER // 16, hc), F32),
            "wz": ((DEPTH, 8, hc), F32),
        }
        for kind, q in (("b", TILE // 4), ("w", INNER // 64)):
            for way in "sr":
                shapes[kind + way + "1"] = ((2, 2, SIDE, q, hc), BF16)
                shapes[kind + way + "2"] = ((2, 2, SIDE, 2 * q, hc), BF16)
                shapes[kind + way + "3"] = ((2, 2, q, hc), BF16)
                shapes[kind + way + "4"] = ((2, 2, 2 * q, hc), BF16)
            shapes[kind + "acc"] = ((2, SIDE, 2 * q, hc), F32)
        for name, (shape, dtype) in shapes.items():
            refs[name + str(k)] = VMEM(shape, dtype)
    return refs


def on_device(tiles, coords, counts, features, weight, grad_out):
    scratch = scratch_of()
    anywhere = pl.BlockSpec(memory_space=pl.ANY)
    shapes = (
        jax.ShapeDtypeStruct((ROWS, WIDE), BF16),
        jax.ShapeDtypeStruct((8, WIDE), F32),
        jax.ShapeDtypeStruct((TILE, WIDE), BF16),
    )
    return pl.pallas_call(
        functools.partial(kernel, tuple(scratch)),
        out_shape=shapes,
        in_specs=[pl.BlockSpec(memory_space=pltpu.SMEM)] + [anywhere] * 4,
        out_specs=(anywhere, pl.BlockSpec(memory_space=VMEM), pl.BlockSpec(memory_space=VMEM)),
        scratch_shapes=list(scratch.values()),
        compiler_params=pltpu.CompilerParams(
            collective_id=0, has_side_effects=True, vmem_limit_bytes=VMEM_LIMIT
        ),
        cost_estimate=pl.CostEstimate(flops=11 * 10**9, bytes_accessed=10 * 2**20, transcendentals=2**20),
        name="graph_layer",
    )(slot_table(coords[0, 0], counts[0, 0]), tiles[0, 0], features, weight, grad_out)

def solution(mesh):
    return jax.shard_map(
        on_device,
        mesh=mesh,
        in_specs=(
            P("row", "col", None, None, None),
            P("row", "col", None, None),
            P("row", "col"),
            P(("col", "row"), None),
            P(None, "feat"),
            P("row", "feat"),
        ),
        out_specs=(P("row", "feat"), P(("row", "col"), "feat"), P(("col", "row"), "feat")),
        check_vma=False,
    )
```

```python
import functools

import jax
import jax.numpy as jnp
from jax import lax
from jax.experimental import pallas as pl
from jax.experimental.pallas import tpu as pltpu
from jax.sharding import PartitionSpec as P

BF16 = jnp.bfloat16
F32 = jnp.float32
MESH = pl.DeviceIdType.MESH
VMEM = pltpu.VMEM

VMEM_LIMIT = 50 * 1024 * 1024
SIDE = 4
DEPTH = 8
TILE = 128
ROWS = 2048
SLAB = ROWS // DEPTH
HALF = SLAB // 2
WIDE = 512
INNER = 1024
WIDTHS = (256, 256)
PARTS = len(WIDTHS)
ORDER = (
    0, 1, 0, 1, 0, 1, 0, 4, 1, 0, 1, 0, 1, 4, 0, 4, 1, 0, 1, 0, 1, 4, 0, 4, 1, 0, 1, 0, 1, 4,
    0, 2, 1, 3, 2, 3, 2, 3, 2, 3, 2, 3, 5,
)
FIRST = [sum(WIDTHS[:k]) for k in range(len(WIDTHS))]
LAST = PARTS - 1
SLOTS = 12

DN_T = (((0,), (0,)), ((), ()))
DN_N = (((1,), (1,)), ((), ()))


def f32dot(a, b, dims=(((1,), (0,)), ((), ()))):
    return lax.dot_general(a, b, dims, preferred_element_type=F32)


def kernel(names, counts, coords_hbm, tiles_hbm, feat_hbm, weight_hbm, gout_hbm, layer_hbm, wgrad, igrad, *refs):
    r = dict(zip(names, refs))
    tiles, adj, feat, weight, gout, layer = (r[n] for n in ("tiles", "adj", "feat", "weight", "gout", "layer"))
    nodes, back, wown, wz, terms_send, terms_recv, table, slot_of = (
        r[n] for n in ("nodes", "back", "wown", "wz", "terms_send", "terms_recv", "table", "slot_of")
    )
    local_sem, out_sem, send_sem, recv_sem = (r[n] for n in ("local_sem", "out_sem", "send_sem", "recv_sem"))
    row = lax.axis_index("row")
    z = lax.axis_index("col")
    f = lax.axis_index("feat")
    y, x = row // SIDE, row % SIDE

    def at(dy, dx, dz):
        return (((y + dy + SIDE) % SIDE) * SIDE + (x + dx + SIDE) % SIDE, (z + dz + DEPTH) % DEPTH, f)

    xp, xm = at(0, 1, 0), at(0, -1, 0)
    yp, ym = at(1, 0, 0), at(-1, 0, 0)
    ways = [xp, xm, yp, ym]
    zpeer = [None] + [at(0, 0, d) for d in range(1, DEPTH)]
    zp, zm = zpeer[1], zpeer[DEPTH - 1]
    other = (row, z, 1 - f)

    def weight_load(k):
        cols = slice(FIRST[k], FIRST[k] + WIDTHS[k])
        return pltpu.make_async_copy(weight_hbm.at[:, cols], weight.at[:, cols], local_sem.at[3 + k])

    coords = r["coords"]
    places = pltpu.make_async_copy(coords_hbm, coords, local_sem.at[4 + PARTS])
    loads = [
        pltpu.make_async_copy(feat_hbm, feat, local_sem.at[0]),
        weight_load(0),
        pltpu.make_async_copy(tiles_hbm, tiles.at[0:TILE], local_sem.at[1]),
        *[weight_load(k) for k in range(1, LAST + 1)],
        pltpu.make_async_copy(gout_hbm, gout, local_sem.at[2]),
    ]
    for load in loads:
        load.start()
    places.start()

    barrier = pltpu.get_barrier_semaphore()
    partners = [xp, xm, yp, ym, other] + zpeer[1:]
    for device in partners:
        pl.semaphore_signal(barrier, inc=1, device_id=device, device_id_type=MESH)

    def send(src, dst, to, slot):
        copy = pltpu.make_async_remote_copy(
            src_ref=src, dst_ref=dst, send_sem=send_sem.at[slot], recv_sem=recv_sem.at[slot],
            device_id=to, device_id_type=MESH,
        )
        copy.start()
        return copy

    def arrive(copies):
        for copy in copies:
            copy.wait_recv()
        for copy in copies:
            copy.wait_send()

    def find_slots():
        shape = (SIDE**4, TILE)
        slot = lax.broadcasted_iota(jnp.int32, shape, 1)
        place = jnp.broadcast_to(coords[0:1] * SIDE**2 + coords[1:2], shape)
        hit = (place == lax.broadcasted_iota(jnp.int32, shape, 0)) & (slot < counts[0, 0])
        found = jnp.where(hit, slot, TILE)
        table[...] = jnp.min(found.T, axis=0, keepdims=True)
        return pltpu.make_async_copy(table, slot_of, local_sem.at[3 + PARTS])

    def lay_out(first, count):
        def one(n, carry):
            slab = first + n // 2
            tile_row = ((z + slab) % DEPTH) * 2 + n % 2
            start = pl.multiple_of((slab * 2 + n % 2) * TILE, TILE)
            for i in range(SIDE):
                for j in range(SIDE):
                    tile_col = ((y + i) % SIDE) * SIDE + (x + j) % SIDE
                    slot = slot_of[0, tile_row * SIDE * SIDE + tile_col]
                    c = (i * SIDE + j) * TILE
                    adj[pl.ds(start, TILE), c : c + TILE] = tiles[slot]
            return carry

        lax.fori_loop(0, 2 * count, one, 0)

    def scatter_sum(kinds, bufs, slot):
        s1, s2, s3, s4, r1, r2, r3, r4, own = bufs
        first, last = ((2, 3), (0, 1)), ((0, 1), (2, 3))

        def send_all(src, dst, to, phase):
            return [
                send(src.at[n, d], dst.at[n, d], ways[to[n][d]], slot + 2 * to[n][d] + phase % 2)
                for n in range(2)
                for d in range(2)
            ]

        def each():
            at_q = 0
            for term, q in kinds:
                for n in range(2):

                    def acc(a, t, lo, hi, n=n, term=term, q=q):
                        return term(a, t, lo, hi) if n == 0 else term(t, a, 2 * q + lo, 2 * q + hi)

                    one, two = slice(at_q, at_q + q), slice(2 * at_q, 2 * (at_q + q))
                    yield n, acc, q, one, two, slice(two.start, two.start + q), slice(two.start + q, two.stop)
                at_q += q

        for n, acc, q, one, two, up, down in each():
            for t in range(SIDE):
                s1[n, 0, t, one] = acc(2, t, 0, q).astype(BF16)
                s1[n, 1, t, one] = acc(2, t, q, 2 * q).astype(BF16)
        c = send_all(s1, r1, first, 0)
        yield
        arrive(c)
        for n, acc, q, one, two, up, down in each():
            for t in range(SIDE):
                s2[n, 0, t, up] = (acc(1, t, 0, q) + r1[n, 0, t, one].astype(F32)).astype(BF16)
                s2[n, 0, t, down] = acc(1, t, q, 2 * q).astype(BF16)
                s2[n, 1, t, up] = acc(3, t, 0, q).astype(BF16)
                s2[n, 1, t, down] = (acc(3, t, q, 2 * q) + r1[n, 1, t, one].astype(F32)).astype(BF16)
        c = send_all(s2, r2, first, 1)
        yield
        arrive(c)

        def add(t):
            for n, acc, q, one, two, up, down in each():
                own[n, t, two] = acc(0, t, 0, 2 * q) + r2[n, 0, t, two].astype(F32) + r2[n, 1, t, two].astype(F32)

        add(2)
        for n, acc, q, one, two, up, down in each():
            s3[n, 0, one] = own[n, 2, up].astype(BF16)
            s3[n, 1, one] = own[n, 2, down].astype(BF16)
        c = send_all(s3, r3, last, 2)
        for t in (1, 3, 0):
            add(t)
        yield
        arrive(c)
        for n, acc, q, one, two, up, down in each():
            s4[n, 0, up] = (own[n, 1, up] + r3[n, 0, one].astype(F32)).astype(BF16)
            s4[n, 0, down] = own[n, 1, down].astype(BF16)
            s4[n, 1, up] = own[n, 3, up].astype(BF16)
            s4[n, 1, down] = (own[n, 3, down] + r3[n, 1, one].astype(F32)).astype(BF16)
        c = send_all(s4, r4, last, 3)
        yield
        arrive(c)
        res = [[None, None] for _ in kinds]
        for m, (n, acc, q, one, two, up, down) in enumerate(each()):
            res[m // 2][n] = own[n, 0, two] + r4[n, 0, two].astype(F32) + r4[n, 1, two].astype(F32)
        return res

    def plane_gather(g, slot):
        h, q = TILE // 2, TILE // 4

        def send_all(phase, *moves):
            return [
                send(src, dst, to, slot + 2 * n + phase % 2)
                for n, (src, dst, to) in enumerate(zip(moves[0::2], moves[1::2], (xp, xm, yp, ym)))
            ]

        own_h, own_l = g.at[0, 0, 0:h], g.at[0, 0, h:TILE]
        c = send_all(
            0, own_h, g.at[0, 3, 0:h], own_h, g.at[0, 1, 0:h],
            own_l, g.at[3, 0, h:TILE], own_l, g.at[1, 0, h:TILE],
        )
        yield
        arrive(c)
        c = send_all(
            1, g.at[0, 3, 0:q], g.at[0, 2, 0:q], g.at[0, 1, q:h], g.at[0, 2, q:h],
            g.at[3, 0, h : h + q], g.at[2, 0, h : h + q], g.at[1, 0, h + q : TILE], g.at[2, 0, h + q : TILE],
        )
        yield
        arrive(c)
        c = send_all(
            2, g.at[:, 0, h:TILE], g.at[:, 3, h:TILE], g.at[:, 0, h:TILE], g.at[:, 1, h:TILE],
            g.at[0, :, 0:h], g.at[3, :, 0:h], g.at[0, :, 0:h], g.at[1, :, 0:h],
        )
        yield
        arrive(c)
        c = send_all(
            3, g.at[:, 3, h : h + q], g.at[:, 2, h : h + q], g.at[:, 1, h + q : TILE], g.at[:, 2, h + q : TILE],
            g.at[3, :, 0:q], g.at[2, :, 0:q], g.at[1, :, q:h], g.at[2, :, q:h],
        )
        yield
        arrive(c)

    def gather_features():
        mine = nodes.at[f]
        for n in range(2):

            @pl.when(f == n)
            def _():
                nodes[n, 0, 0] = feat[:, n * WIDE : (n + 1) * WIDE]

        yield from plane_gather(mine, SLOTS * PARTS)
        c = [send(mine, nodes.at[f], other, SLOTS * PARTS + 8)]
        yield
        arrive(c)

    def flow(k):
        hc, slot = WIDTHS[k], SLOTS * k
        cols = slice(FIRST[k], FIRST[k] + hc)
        g, part, pre, delta, bsum, bpart = (r[n + str(k)] for n in ("gath", "part", "pre", "delta", "bsum", "bpart"))
        zsend_p, zsend_m, zrecv_p, zrecv_m = (r[n + str(k)] for n in ("zsend_p", "zsend_m", "zrecv_p", "zrecv_m"))

        if k == 0:
            loads[0].wait()
        loads[1 if k == 0 else 2 + k].wait()
        g[0, 0] = f32dot(feat[...], weight[:, cols]).astype(BF16)
        if k == 0:
            pl.semaphore_wait(barrier, len(partners))
        gather = plane_gather(g, slot)
        next(gather)
        if k == 0:
            places.wait()
            found = find_slots()
            found.start()
            found.wait()
            loads[2].wait()
            tiles[TILE] = jnp.zeros((TILE, TILE), BF16)
            lay_out(3, 3)
        yield
        next(gather)
        if k == 0:
            lay_out(0, 3)
            lay_out(6, 2)
        yield
        yield from gather

        def slabs(first, last):
            value = f32dot(adj[first * SLAB : last * SLAB, :], g[...].reshape(ROWS, hc))
            part[first:last] = value.reshape(last - first, SLAB, hc)

        def send_z(step, up, down):
            return [send(*up, zp, slot + 8 + step % 2), send(*down, zm, slot + 10 + step % 2)]

        top, low = slice(0, HALF), slice(HALF, SLAB)
        slabs(3, 6)
        zsend_p[0, top] = part[4, top].astype(BF16)
        zsend_p[0, low] = part[3, low].astype(BF16)
        zsend_m[0, top] = part[5, top].astype(BF16)
        zsend_m[0, low] = part[4, low].astype(BF16)
        c = send_z(0, (zsend_p.at[0], zrecv_p.at[0]), (zsend_m.at[0], zrecv_m.at[0]))
        slabs(6, 8)
        slabs(0, 3)
        yield
        for s in (1, 2):
            arrive(c)
            zsend_p[s, top] = (part[4 - s, top] + zrecv_p[s - 1, top].astype(F32)).astype(BF16)
            zsend_p[s, low] = (part[3 - s, low] + zrecv_p[s - 1, low].astype(F32)).astype(BF16)
            zsend_m[s, top] = (part[5 + s, top] + zrecv_m[s - 1, top].astype(F32)).astype(BF16)
            zsend_m[s, low] = (part[4 + s, low] + zrecv_m[s - 1, low].astype(F32)).astype(BF16)
            c = send_z(s, (zsend_p.at[s], zrecv_p.at[s]), (zsend_m.at[s], zrecv_m.at[s]))
            yield
        arrive(c)
        zsend_p[3, top] = (part[1, top] + zrecv_p[2, top].astype(F32)).astype(BF16)
        zsend_m[3, low] = (part[7, low] + zrecv_m[2, low].astype(F32)).astype(BF16)
        c = send_z(3, (zsend_p.at[3, top], zrecv_p.at[3, top]), (zsend_m.at[3, low], zrecv_m.at[3, low]))
        yield
        arrive(c)
        pre[0, top] = (part[0, top] + zrecv_m[2, top].astype(F32) + zrecv_p[3, top].astype(F32)).astype(BF16)
        pre[0, low] = (part[0, low] + zrecv_p[2, low].astype(F32) + zrecv_m[3, low].astype(F32)).astype(BF16)

        def activate(i):
            start = pl.multiple_of(((z + i) % DEPTH) * SLAB, SLAB)
            value = pre[i].astype(F32)
            sig = 0.5 + 0.5 * jnp.tanh(0.5 * value)
            layer[pl.ds(start, SLAB), cols] = (value * sig).astype(BF16)
            slope = sig * (1.0 + value * (1.0 - sig))
            delta[i * SLAB : (i + 1) * SLAB] = (gout[pl.ds(start, SLAB), cols].astype(F32) * slope).astype(BF16)

        c = send_z(4, (pre.at[0], pre.at[7]), (pre.at[0], pre.at[1]))
        if k == 0:
            loads[-1].wait()
        activate(0)
        yield
        for s in (1, 2):
            arrive(c)
            c = send_z(4 + s, (pre.at[8 - s], pre.at[7 - s]), (pre.at[s], pre.at[s + 1]))
            activate(8 - s)
            activate(s)
            yield
        arrive(c)
        c = send_z(7, (pre.at[5, top], pre.at[4, top]), (pre.at[3, low], pre.at[4, low]))
        activate(5)
        activate(3)
        for n in range(DEPTH):
            c0 = n * SLAB
            bsum[c0 : c0 + SLAB] = f32dot(adj[0 : 4 * SLAB, c0 : c0 + SLAB], delta[0 : 4 * SLAB], DN_T) + f32dot(
                adj[5 * SLAB :, c0 : c0 + SLAB], delta[5 * SLAB :], DN_T
            )
        yield
        arrive(c)
        activate(4)
        mid = slice(4 * SLAB, 5 * SLAB)
        for n in (4, 5, 0, 1, 2, 3, 6, 7):
            c0 = n * SLAB
            value = bsum[c0 : c0 + SLAB] + f32dot(adj[mid, c0 : c0 + SLAB], delta[mid], DN_T)
            bpart[n // 2, n % 2 * 2 : n % 2 * 2 + 2] = value.astype(BF16).reshape(2, TILE, hc)
        out = pltpu.make_async_copy(layer.at[:, cols], layer_hbm.at[:, cols], out_sem.at[k])
        out.start()
        outs.append(out)

    def plane_sums(k):
        hc = WIDTHS[k]
        cols = slice(FIRST[k], FIRST[k] + hc)
        bpart, wpart = r["bpart" + str(k)], r["wpart" + str(k)]
        block = bpart[...].reshape(ROWS, hc)
        for n in range(2):
            value = f32dot(nodes[n].reshape(ROWS, WIDE), block, DN_T)
            wpart[n * WIDE : (n + 1) * WIDE] = value * ((ROWS * DEPTH) ** -0.5)

        def bterm(i, j, lo, hi):
            return bpart[i, j, lo:hi].astype(F32)

        def wterm(i, j, lo, hi):
            start = (((y + i) % SIDE) * SIDE + (x + j) % SIDE) * (INNER // 16) + lo
            return wpart[pl.ds(pl.multiple_of(start, 16), hi - lo)]

        bufs = [r["sum_" + n + str(k)] for n in ("s1", "s2", "s3", "s4", "r1", "r2", "r3", "r4", "own")]
        res = yield from scatter_sum(((bterm, TILE // 4), (wterm, INNER // 64)), bufs, SLOTS * k)
        for n in range(2):
            wown[n * 32 : (n + 1) * 32, cols] = res[1][n]
            back[n * TILE // 2 : (n + 1) * TILE // 2, cols] = res[0][n].astype(BF16)

    def finish():
        slot = SLOTS * PARTS + 9
        for d in range(1, DEPTH):
            start = pl.multiple_of(((z + d) % DEPTH) * 8, 8)
            send(wown.at[pl.ds(start, 8)], wz.at[d], zpeer[d], slot)
        theirs = f32dot(back[...], weight[pl.ds(pl.multiple_of((1 - f) * WIDE, WIDE), WIDE)], DN_N)
        terms_send[...] = theirs.astype(BF16)
        swap = [send(terms_send, terms_recv, other, slot + 1)]
        mine = f32dot(back[...], weight[pl.ds(pl.multiple_of(f * WIDE, WIDE), WIDE)], DN_N)
        total = wown[pl.ds(pl.multiple_of(z * 8, 8), 8)]
        arrive(swap)
        igrad[...] = (mine + terms_recv[...].astype(F32)).astype(BF16)
        others = wz.at[1:DEPTH]
        pltpu.make_async_copy(others, others, recv_sem.at[slot]).wait()
        pltpu.make_async_copy(others, others, send_sem.at[slot]).wait()
        for d in range(1, DEPTH):
            total = total + wz[d]
        wgrad[...] = total
        yield

    outs = []
    flows = [make(k) for make in (flow, plane_sums) for k in range(PARTS)] + [gather_features(), finish()]
    for n in ORDER:
        next(flows[n], None)
    for out in outs:
        out.wait()


def scratch_of():
    dma = pltpu.SemaphoreType.DMA
    slots = SLOTS * PARTS + 11
    refs = {
        "tiles": VMEM((TILE + 1, TILE, TILE), BF16),
        "adj": VMEM((ROWS, ROWS), BF16),
        "feat": VMEM((TILE, INNER), BF16),
        "weight": VMEM((INNER, WIDE), BF16),
        "gout": VMEM((ROWS, WIDE), BF16),
        "layer": VMEM((ROWS, WIDE), BF16),
        "nodes": VMEM((2, SIDE, SIDE, TILE, WIDE), BF16),
        "back": VMEM((TILE, WIDE), BF16),
        "wown": VMEM((INNER // 16, WIDE), F32),
        "wz": VMEM((DEPTH, 8, WIDE), F32),
        "coords": VMEM((2, TILE), jnp.int32),
        "table": VMEM((1, SIDE**4), jnp.int32),
        "slot_of": pltpu.SMEM((1, SIDE**4), jnp.int32),
        "terms_send": VMEM((TILE, WIDE), BF16),
        "terms_recv": VMEM((TILE, WIDE), BF16),
        "local_sem": dma((5 + PARTS,)),
        "out_sem": dma((PARTS,)),
        "send_sem": dma((slots,)),
        "recv_sem": dma((slots,)),
    }
    for k, hc in enumerate(WIDTHS):
        shapes = {
            "gath": ((SIDE, SIDE, TILE, hc), BF16),
            "part": ((DEPTH, SLAB, hc), F32),
            "zsend_p": ((4, SLAB, hc), BF16),
            "zsend_m": ((4, SLAB, hc), BF16),
            "zrecv_p": ((4, SLAB, hc), BF16),
            "zrecv_m": ((4, SLAB, hc), BF16),
            "pre": ((DEPTH, SLAB, hc), BF16),
            "delta": ((ROWS, hc), BF16),
            "bsum": ((ROWS, hc), F32),
            "bpart": ((SIDE, SIDE, TILE, hc), BF16),
            "wpart": ((INNER, hc), F32),
        }
        q = TILE // 4 + INNER // 64
        for way in "sr":
            shapes["sum_" + way + "1"] = ((2, 2, SIDE, q, hc), BF16)
            shapes["sum_" + way + "2"] = ((2, 2, SIDE, 2 * q, hc), BF16)
            shapes["sum_" + way + "3"] = ((2, 2, q, hc), BF16)
            shapes["sum_" + way + "4"] = ((2, 2, 2 * q, hc), BF16)
        shapes["sum_own"] = ((2, SIDE, 2 * q, hc), F32)
        for name, (shape, dtype) in shapes.items():
            refs[name + str(k)] = VMEM(shape, dtype)
    return refs


def on_device(tiles, coords, counts, features, weight, grad_out):
    scratch = scratch_of()
    anywhere, hbm = pl.BlockSpec(memory_space=pl.ANY), pl.BlockSpec(memory_space=pltpu.HBM)
    shapes = (
        jax.ShapeDtypeStruct((ROWS, WIDE), BF16),
        jax.ShapeDtypeStruct((8, WIDE), F32),
        jax.ShapeDtypeStruct((TILE, WIDE), BF16),
    )
    return pl.pallas_call(
        functools.partial(kernel, tuple(scratch)),
        out_shape=shapes,
        in_specs=[pl.BlockSpec(memory_space=pltpu.SMEM)] + [hbm] * 5,
        out_specs=(anywhere, pl.BlockSpec(memory_space=VMEM), pl.BlockSpec(memory_space=VMEM)),
        scratch_shapes=list(scratch.values()),
        compiler_params=pltpu.CompilerParams(
            collective_id=0, has_side_effects=True, vmem_limit_bytes=VMEM_LIMIT
        ),
        cost_estimate=pl.CostEstimate(flops=11 * 10**9, bytes_accessed=10 * 2**20, transcendentals=2**20),
        name="graph_layer",
    )(counts, coords[0, 0].T, tiles[0, 0], features, weight, grad_out)

def solution(mesh):
    return jax.shard_map(
        on_device,
        mesh=mesh,
        in_specs=(
            P("row", "col", None, None, None),
            P("row", "col", None, None),
            P("row", "col"),
            P(("col", "row"), None),
            P(None, "feat"),
            P("row", "feat"),
        ),
        out_specs=(P("row", "feat"), P(("row", "col"), "feat"), P(("col", "row"), "feat")),
        check_vma=False,
    )
```

```python
import functools

import jax
import jax.numpy as jnp
from jax import lax
from jax.experimental import pallas as pl
from jax.experimental.pallas import tpu as pltpu
from jax.sharding import PartitionSpec as P

BF16 = jnp.bfloat16
F32 = jnp.float32
MESH = pl.DeviceIdType.MESH
VMEM = pltpu.VMEM

VMEM_LIMIT = 50 * 1024 * 1024
SIDE = 4
DEPTH = 8
TILE = 128
ROWS = 2048
SLAB = ROWS // DEPTH
HALF = SLAB // 2
WIDE = 512
INNER = 1024
WIDTHS = (256, 256)
PARTS = len(WIDTHS)
CUTS = (1, 2)
ORDER = (
    0, 1, 0, 1, 0, 1, 0, 5, 1, 0, 1, 5, 0, 1, 5, 0, 1, 0, 5, 1, 0, 1, 0, 1, 5, 0, 1, 0, 1, 5,
    0, 2, 1, 3, 4, 2, 4, 3, 2, 4, 3, 2, 4, 3, 2, 4, 3, 6,
)
FIRST = [sum(WIDTHS[:k]) for k in range(len(WIDTHS))]
LAST = PARTS - 1
PIECES = [(k, n) for k in range(PARTS) for n in range(CUTS[k])]
LATER = [p for p in PIECES if p[1] > 0]
SLOTS = 12

DN_T = (((0,), (0,)), ((), ()))
DN_N = (((1,), (1,)), ((), ()))


def f32dot(a, b, dims=(((1,), (0,)), ((), ()))):
    return lax.dot_general(a, b, dims, preferred_element_type=F32)


def kernel(names, counts, coords_hbm, tiles_hbm, feat_hbm, weight_hbm, gout_hbm, layer_hbm, wgrad, igrad, *refs):
    r = dict(zip(names, refs))
    tiles, adj, feat, weight, gout, layer = (r[n] for n in ("tiles", "adj", "feat", "weight", "gout", "layer"))
    nodes, back, wown, wz, terms_send, terms_recv, table, slot_of = (
        r[n] for n in ("nodes", "back", "wown", "wz", "terms_send", "terms_recv", "table", "slot_of")
    )
    local_sem, out_sem, send_sem, recv_sem = (r[n] for n in ("local_sem", "out_sem", "send_sem", "recv_sem"))
    row = lax.axis_index("row")
    z = lax.axis_index("col")
    f = lax.axis_index("feat")
    y, x = row // SIDE, row % SIDE

    def at(dy, dx, dz):
        return (((y + dy + SIDE) % SIDE) * SIDE + (x + dx + SIDE) % SIDE, (z + dz + DEPTH) % DEPTH, f)

    xp, xm = at(0, 1, 0), at(0, -1, 0)
    yp, ym = at(1, 0, 0), at(-1, 0, 0)
    ways = [xp, xm, yp, ym]
    zpeer = [None] + [at(0, 0, d) for d in range(1, DEPTH)]
    zp, zm = zpeer[1], zpeer[DEPTH - 1]
    other = (row, z, 1 - f)

    def weight_load(k):
        cols = slice(FIRST[k], FIRST[k] + WIDTHS[k])
        return pltpu.make_async_copy(weight_hbm.at[:, cols], weight.at[:, cols], local_sem.at[3 + k])

    coords = r["coords"]
    places = pltpu.make_async_copy(coords_hbm, coords, local_sem.at[4 + PARTS])
    loads = [
        pltpu.make_async_copy(feat_hbm, feat, local_sem.at[0]),
        weight_load(0),
        pltpu.make_async_copy(tiles_hbm, tiles.at[0:TILE], local_sem.at[1]),
        *[weight_load(k) for k in range(1, LAST + 1)],
        pltpu.make_async_copy(gout_hbm, gout, local_sem.at[2]),
    ]
    for load in loads:
        load.start()
    places.start()

    barrier = pltpu.get_barrier_semaphore()
    partners = [xp, xm, yp, ym, other] + zpeer[1:]
    for device in partners:
        pl.semaphore_signal(barrier, inc=1, device_id=device, device_id_type=MESH)

    def send(src, dst, to, slot):
        copy = pltpu.make_async_remote_copy(
            src_ref=src, dst_ref=dst, send_sem=send_sem.at[slot], recv_sem=recv_sem.at[slot],
            device_id=to, device_id_type=MESH,
        )
        copy.start()
        return copy

    def arrive(copies):
        for copy in copies:
            copy.wait_recv()
        for copy in copies:
            copy.wait_send()

    def find_slots():
        shape = (SIDE**4, TILE)
        slot = lax.broadcasted_iota(jnp.int32, shape, 1)
        place = jnp.broadcast_to(coords[0:1] * SIDE**2 + coords[1:2], shape)
        hit = (place == lax.broadcasted_iota(jnp.int32, shape, 0)) & (slot < counts[0, 0])
        found = jnp.where(hit, slot, TILE)
        table[...] = jnp.min(found.T, axis=0, keepdims=True)
        return pltpu.make_async_copy(table, slot_of, local_sem.at[3 + PARTS])

    def lay_out(first, count):
        def one(n, carry):
            slab = first + n // 2
            tile_row = ((z + slab) % DEPTH) * 2 + n % 2
            start = pl.multiple_of((slab * 2 + n % 2) * TILE, TILE)
            for i in range(SIDE):
                for j in range(SIDE):
                    tile_col = ((y + i) % SIDE) * SIDE + (x + j) % SIDE
                    slot = slot_of[0, tile_row * SIDE * SIDE + tile_col]
                    c = (i * SIDE + j) * TILE
                    adj[pl.ds(start, TILE), c : c + TILE] = tiles[slot]
            return carry

        lax.fori_loop(0, 2 * count, one, 0)

    def scatter_sum(kinds, bufs, slot):
        s1, s2, s3, s4, r1, r2, r3, r4, own = bufs
        first, last = ((2, 3), (0, 1)), ((0, 1), (2, 3))

        def send_all(src, dst, to, phase):
            return [
                send(src.at[n, d], dst.at[n, d], ways[to[n][d]], slot + 2 * to[n][d] + phase % 2)
                for n in range(2)
                for d in range(2)
            ]

        def each():
            at_q = 0
            for term, q in kinds:
                for n in range(2):

                    def acc(a, t, lo, hi, n=n, term=term, q=q):
                        return term(a, t, lo, hi) if n == 0 else term(t, a, 2 * q + lo, 2 * q + hi)

                    one, two = slice(at_q, at_q + q), slice(2 * at_q, 2 * (at_q + q))
                    yield n, acc, q, one, two, slice(two.start, two.start + q), slice(two.start + q, two.stop)
                at_q += q

        for n, acc, q, one, two, up, down in each():
            for t in range(SIDE):
                s1[n, 0, t, one] = acc(2, t, 0, q).astype(BF16)
                s1[n, 1, t, one] = acc(2, t, q, 2 * q).astype(BF16)
        c = send_all(s1, r1, first, 0)
        yield
        arrive(c)
        for n, acc, q, one, two, up, down in each():
            for t in range(SIDE):
                s2[n, 0, t, up] = (acc(1, t, 0, q) + r1[n, 0, t, one].astype(F32)).astype(BF16)
                s2[n, 0, t, down] = acc(1, t, q, 2 * q).astype(BF16)
                s2[n, 1, t, up] = acc(3, t, 0, q).astype(BF16)
                s2[n, 1, t, down] = (acc(3, t, q, 2 * q) + r1[n, 1, t, one].astype(F32)).astype(BF16)
        c = send_all(s2, r2, first, 1)
        yield
        arrive(c)

        def add(t):
            for n, acc, q, one, two, up, down in each():
                own[n, t, two] = acc(0, t, 0, 2 * q) + r2[n, 0, t, two].astype(F32) + r2[n, 1, t, two].astype(F32)

        add(2)
        for n, acc, q, one, two, up, down in each():
            s3[n, 0, one] = own[n, 2, up].astype(BF16)
            s3[n, 1, one] = own[n, 2, down].astype(BF16)
        c = send_all(s3, r3, last, 2)
        for t in (1, 3, 0):
            add(t)
        yield
        arrive(c)
        for n, acc, q, one, two, up, down in each():
            s4[n, 0, up] = (own[n, 1, up] + r3[n, 0, one].astype(F32)).astype(BF16)
            s4[n, 0, down] = own[n, 1, down].astype(BF16)
            s4[n, 1, up] = own[n, 3, up].astype(BF16)
            s4[n, 1, down] = (own[n, 3, down] + r3[n, 1, one].astype(F32)).astype(BF16)
        c = send_all(s4, r4, last, 3)
        yield
        arrive(c)
        res = [[None, None] for _ in kinds]
        for m, (n, acc, q, one, two, up, down) in enumerate(each()):
            res[m // 2][n] = own[n, 0, two] + r4[n, 0, two].astype(F32) + r4[n, 1, two].astype(F32)
        return res

    def plane_gather(g, slot):
        h, q = TILE // 2, TILE // 4

        def send_all(phase, *moves):
            return [
                send(src, dst, to, slot + 2 * n + phase % 2)
                for n, (src, dst, to) in enumerate(zip(moves[0::2], moves[1::2], (xp, xm, yp, ym)))
            ]

        own_h, own_l = g.at[0, 0, 0:h], g.at[0, 0, h:TILE]
        c = send_all(
            0, own_h, g.at[0, 3, 0:h], own_h, g.at[0, 1, 0:h],
            own_l, g.at[3, 0, h:TILE], own_l, g.at[1, 0, h:TILE],
        )
        yield
        arrive(c)
        c = send_all(
            1, g.at[0, 3, 0:q], g.at[0, 2, 0:q], g.at[0, 1, q:h], g.at[0, 2, q:h],
            g.at[3, 0, h : h + q], g.at[2, 0, h : h + q], g.at[1, 0, h + q : TILE], g.at[2, 0, h + q : TILE],
        )
        yield
        arrive(c)
        c = send_all(
            2, g.at[:, 0, h:TILE], g.at[:, 3, h:TILE], g.at[:, 0, h:TILE], g.at[:, 1, h:TILE],
            g.at[0, :, 0:h], g.at[3, :, 0:h], g.at[0, :, 0:h], g.at[1, :, 0:h],
        )
        yield
        arrive(c)
        c = send_all(
            3, g.at[:, 3, h : h + q], g.at[:, 2, h : h + q], g.at[:, 1, h + q : TILE], g.at[:, 2, h + q : TILE],
            g.at[3, :, 0:q], g.at[2, :, 0:q], g.at[1, :, q:h], g.at[2, :, q:h],
        )
        yield
        arrive(c)

    def gather_features():
        mine = nodes.at[f]
        for n in range(2):

            @pl.when(f == n)
            def _():
                nodes[n, 0, 0] = feat[:, n * WIDE : (n + 1) * WIDE]

        yield from plane_gather(mine, SLOTS * PARTS)
        c = [send(mine, nodes.at[f], other, SLOTS * PARTS + 8)]
        yield
        arrive(c)

    def flow(k):
        hc, slot = WIDTHS[k], SLOTS * k
        cols = slice(FIRST[k], FIRST[k] + hc)
        g, part, pre, delta, bsum, bpart = (r[n + str(k)] for n in ("gath", "part", "pre", "delta", "bsum", "bpart"))
        zsend_p, zsend_m, zrecv_p, zrecv_m = (r[n + str(k)] for n in ("zsend_p", "zsend_m", "zrecv_p", "zrecv_m"))

        if k == 0:
            loads[0].wait()
        loads[1 if k == 0 else 2 + k].wait()
        g[0, 0] = f32dot(feat[...], weight[:, cols]).astype(BF16)
        if k == 0:
            pl.semaphore_wait(barrier, len(partners))
        gather = plane_gather(g, slot)
        next(gather)
        if k == 0:
            places.wait()
            found = find_slots()
            found.start()
            found.wait()
            loads[2].wait()
            tiles[TILE] = jnp.zeros((TILE, TILE), BF16)
            lay_out(3, 3)
        yield
        next(gather)
        if k == 0:
            lay_out(0, 3)
            lay_out(6, 2)
        yield
        yield from gather

        def slabs(first, last):
            value = f32dot(adj[first * SLAB : last * SLAB, :], g[...].reshape(ROWS, hc))
            part[first:last] = value.reshape(last - first, SLAB, hc)

        def send_z(step, up, down):
            return [send(*up, zp, slot + 8 + step % 2), send(*down, zm, slot + 10 + step % 2)]

        top, low = slice(0, HALF), slice(HALF, SLAB)
        slabs(3, 6)
        zsend_p[0, top] = part[4, top].astype(BF16)
        zsend_p[0, low] = part[3, low].astype(BF16)
        zsend_m[0, top] = part[5, top].astype(BF16)
        zsend_m[0, low] = part[4, low].astype(BF16)
        c = send_z(0, (zsend_p.at[0], zrecv_p.at[0]), (zsend_m.at[0], zrecv_m.at[0]))
        slabs(6, 8)
        slabs(0, 3)
        yield
        for s in (1, 2):
            arrive(c)
            zsend_p[s, top] = (part[4 - s, top] + zrecv_p[s - 1, top].astype(F32)).astype(BF16)
            zsend_p[s, low] = (part[3 - s, low] + zrecv_p[s - 1, low].astype(F32)).astype(BF16)
            zsend_m[s, top] = (part[5 + s, top] + zrecv_m[s - 1, top].astype(F32)).astype(BF16)
            zsend_m[s, low] = (part[4 + s, low] + zrecv_m[s - 1, low].astype(F32)).astype(BF16)
            c = send_z(s, (zsend_p.at[s], zrecv_p.at[s]), (zsend_m.at[s], zrecv_m.at[s]))
            yield
        arrive(c)
        zsend_p[3, top] = (part[1, top] + zrecv_p[2, top].astype(F32)).astype(BF16)
        zsend_m[3, low] = (part[7, low] + zrecv_m[2, low].astype(F32)).astype(BF16)
        c = send_z(3, (zsend_p.at[3, top], zrecv_p.at[3, top]), (zsend_m.at[3, low], zrecv_m.at[3, low]))
        yield
        arrive(c)
        pre[0, top] = (part[0, top] + zrecv_m[2, top].astype(F32) + zrecv_p[3, top].astype(F32)).astype(BF16)
        pre[0, low] = (part[0, low] + zrecv_p[2, low].astype(F32) + zrecv_m[3, low].astype(F32)).astype(BF16)

        def activate(i):
            start = pl.multiple_of(((z + i) % DEPTH) * SLAB, SLAB)
            value = pre[i].astype(F32)
            sig = 0.5 + 0.5 * jnp.tanh(0.5 * value)
            layer[pl.ds(start, SLAB), cols] = (value * sig).astype(BF16)
            slope = sig * (1.0 + value * (1.0 - sig))
            delta[i * SLAB : (i + 1) * SLAB] = (gout[pl.ds(start, SLAB), cols].astype(F32) * slope).astype(BF16)

        c = send_z(4, (pre.at[0], pre.at[7]), (pre.at[0], pre.at[1]))
        if k == 0:
            loads[-1].wait()
        activate(0)
        yield
        for s in (1, 2):
            arrive(c)
            c = send_z(4 + s, (pre.at[8 - s], pre.at[7 - s]), (pre.at[s], pre.at[s + 1]))
            activate(8 - s)
            activate(s)
            yield
        arrive(c)
        c = send_z(7, (pre.at[5, top], pre.at[4, top]), (pre.at[3, low], pre.at[4, low]))
        activate(5)
        activate(3)
        for n in range(DEPTH):
            c0 = n * SLAB
            bsum[c0 : c0 + SLAB] = f32dot(adj[0 : 4 * SLAB, c0 : c0 + SLAB], delta[0 : 4 * SLAB], DN_T) + f32dot(
                adj[5 * SLAB :, c0 : c0 + SLAB], delta[5 * SLAB :], DN_T
            )
        yield
        arrive(c)
        activate(4)
        mid = slice(4 * SLAB, 5 * SLAB)
        for n in (4, 5, 0, 1, 2, 3, 6, 7):
            c0 = n * SLAB
            value = bsum[c0 : c0 + SLAB] + f32dot(adj[mid, c0 : c0 + SLAB], delta[mid], DN_T)
            bpart[n // 2, n % 2 * 2 : n % 2 * 2 + 2] = value.astype(BF16).reshape(2, TILE, hc)
        out = pltpu.make_async_copy(layer.at[:, cols], layer_hbm.at[:, cols], out_sem.at[k])
        out.start()
        outs.append(out)

    def plane_sums(k, piece):
        hc = WIDTHS[k]
        wide = hc // CUTS[k]
        inner = slice(piece * wide, (piece + 1) * wide)
        cols = slice(FIRST[k] + inner.start, FIRST[k] + inner.stop)
        bpart, wpart = r["bpart" + str(k)], r["wpart" + str(k)]
        if piece == 0:
            block = bpart[...].reshape(ROWS, hc)
            for n in range(2):
                value = f32dot(nodes[n].reshape(ROWS, WIDE), block, DN_T)
                wpart[n * WIDE : (n + 1) * WIDE] = value * ((ROWS * DEPTH) ** -0.5)

        def bterm(i, j, lo, hi):
            return bpart[i, j, lo:hi, inner].astype(F32)

        def wterm(i, j, lo, hi):
            start = (((y + i) % SIDE) * SIDE + (x + j) % SIDE) * (INNER // 16) + lo
            return wpart[pl.ds(pl.multiple_of(start, 16), hi - lo), inner]

        bufs = [r["sum_" + n + str(k) + str(piece)] for n in ("s1", "s2", "s3", "s4", "r1", "r2", "r3", "r4", "own")]
        res = yield from scatter_sum(((bterm, TILE // 4), (wterm, INNER // 64)), bufs, SLOTS * k if piece == 0 else SLOTS * PARTS + 11 + 8 * LATER.index((k, piece)))
        for n in range(2):
            wown[n * 32 : (n + 1) * 32, cols] = res[1][n]
            back[n * TILE // 2 : (n + 1) * TILE // 2, cols] = res[0][n].astype(BF16)

    def finish():
        slot = SLOTS * PARTS + 9
        for d in range(1, DEPTH):
            start = pl.multiple_of(((z + d) % DEPTH) * 8, 8)
            send(wown.at[pl.ds(start, 8)], wz.at[d], zpeer[d], slot)
        theirs = f32dot(back[...], weight[pl.ds(pl.multiple_of((1 - f) * WIDE, WIDE), WIDE)], DN_N)
        terms_send[...] = theirs.astype(BF16)
        swap = [send(terms_send, terms_recv, other, slot + 1)]
        mine = f32dot(back[...], weight[pl.ds(pl.multiple_of(f * WIDE, WIDE), WIDE)], DN_N)
        total = wown[pl.ds(pl.multiple_of(z * 8, 8), 8)]
        arrive(swap)
        igrad[...] = (mine + terms_recv[...].astype(F32)).astype(BF16)
        others = wz.at[1:DEPTH]
        pltpu.make_async_copy(others, others, recv_sem.at[slot]).wait()
        pltpu.make_async_copy(others, others, send_sem.at[slot]).wait()
        for d in range(1, DEPTH):
            total = total + wz[d]
        wgrad[...] = total
        yield

    outs = []
    flows = [flow(k) for k in range(PARTS)] + [plane_sums(k, n) for k, n in PIECES] + [gather_features(), finish()]
    for n in ORDER:
        next(flows[n], None)
    for out in outs:
        out.wait()


def scratch_of():
    dma = pltpu.SemaphoreType.DMA
    slots = SLOTS * PARTS + 11 + 8 * len(LATER)
    refs = {
        "tiles": VMEM((TILE + 1, TILE, TILE), BF16),
        "adj": VMEM((ROWS, ROWS), BF16),
        "feat": VMEM((TILE, INNER), BF16),
        "weight": VMEM((INNER, WIDE), BF16),
        "gout": VMEM((ROWS, WIDE), BF16),
        "layer": VMEM((ROWS, WIDE), BF16),
        "nodes": VMEM((2, SIDE, SIDE, TILE, WIDE), BF16),
        "back": VMEM((TILE, WIDE), BF16),
        "wown": VMEM((INNER // 16, WIDE), F32),
        "wz": VMEM((DEPTH, 8, WIDE), F32),
        "coords": VMEM((2, TILE), jnp.int32),
        "table": VMEM((1, SIDE**4), jnp.int32),
        "slot_of": pltpu.SMEM((1, SIDE**4), jnp.int32),
        "terms_send": VMEM((TILE, WIDE), BF16),
        "terms_recv": VMEM((TILE, WIDE), BF16),
        "local_sem": dma((5 + PARTS,)),
        "out_sem": dma((PARTS,)),
        "send_sem": dma((slots,)),
        "recv_sem": dma((slots,)),
    }
    for k, hc in enumerate(WIDTHS):
        shapes = {
            "gath": ((SIDE, SIDE, TILE, hc), BF16),
            "part": ((DEPTH, SLAB, hc), F32),
            "zsend_p": ((4, SLAB, hc), BF16),
            "zsend_m": ((4, SLAB, hc), BF16),
            "zrecv_p": ((4, SLAB, hc), BF16),
            "zrecv_m": ((4, SLAB, hc), BF16),
            "pre": ((DEPTH, SLAB, hc), BF16),
            "delta": ((ROWS, hc), BF16),
            "bsum": ((ROWS, hc), F32),
            "bpart": ((SIDE, SIDE, TILE, hc), BF16),
            "wpart": ((INNER, hc), F32),
        }
        q, wide = TILE // 4 + INNER // 64, hc // CUTS[k]
        for piece in range(CUTS[k]):
            for way in "sr":
                shapes[f"sum_{way}1{k}{piece}"] = ((2, 2, SIDE, q, wide), BF16)
                shapes[f"sum_{way}2{k}{piece}"] = ((2, 2, SIDE, 2 * q, wide), BF16)
                shapes[f"sum_{way}3{k}{piece}"] = ((2, 2, q, wide), BF16)
                shapes[f"sum_{way}4{k}{piece}"] = ((2, 2, 2 * q, wide), BF16)
            shapes[f"sum_own{k}{piece}"] = ((2, SIDE, 2 * q, wide), F32)
        for name, (shape, dtype) in shapes.items():
            refs[name if name.startswith("sum_") else name + str(k)] = VMEM(shape, dtype)
    return refs


def on_device(tiles, coords, counts, features, weight, grad_out):
    scratch = scratch_of()
    anywhere, hbm = pl.BlockSpec(memory_space=pl.ANY), pl.BlockSpec(memory_space=pltpu.HBM)
    shapes = (
        jax.ShapeDtypeStruct((ROWS, WIDE), BF16),
        jax.ShapeDtypeStruct((8, WIDE), F32),
        jax.ShapeDtypeStruct((TILE, WIDE), BF16),
    )
    large = (coords[0, 0].T, tiles[0, 0], features, weight, grad_out)
    return pl.pallas_call(
        functools.partial(kernel, tuple(scratch)),
        out_shape=shapes,
        in_specs=[pl.BlockSpec(memory_space=pltpu.SMEM)] + [hbm] * 5,
        out_specs=(anywhere, pl.BlockSpec(memory_space=VMEM), pl.BlockSpec(memory_space=VMEM)),
        scratch_shapes=list(scratch.values()),
        compiler_params=pltpu.CompilerParams(
            collective_id=0, has_side_effects=True, vmem_limit_bytes=VMEM_LIMIT
        ),
        cost_estimate=pl.CostEstimate(flops=11 * 10**9, bytes_accessed=10 * 2**20, transcendentals=2**20),
        name="graph_layer",
    )(counts, *[pltpu.with_memory_space_constraint(v, pltpu.HBM) for v in large])

def solution(mesh):
    return jax.shard_map(
        on_device,
        mesh=mesh,
        in_specs=(
            P("row", "col", None, None, None),
            P("row", "col", None, None),
            P("row", "col"),
            P(("col", "row"), None),
            P(None, "feat"),
            P("row", "feat"),
        ),
        out_specs=(P("row", "feat"), P(("row", "col"), "feat"), P(("col", "row"), "feat")),
        check_vma=False,
    )
```

```python
import functools

import jax
import jax.numpy as jnp
from jax import lax
from jax.experimental import pallas as pl
from jax.experimental.pallas import tpu as pltpu
from jax.sharding import PartitionSpec as P

BF16 = jnp.bfloat16
F32 = jnp.float32
MESH = pl.DeviceIdType.MESH
VMEM = pltpu.VMEM

VMEM_LIMIT = 50 * 1024 * 1024
SIDE = 4
DEPTH = 8
TILE = 128
ROWS = 2048
SLAB = ROWS // DEPTH
HALF = SLAB // 2
WIDE = 512
INNER = 1024
WIDTHS = (256, 256)
PARTS = len(WIDTHS)
CUTS = (1, 2)
ORDER = (
    0, 1, 0, 1, 0, 1, 0, 5, 1, 0, 1, 5, 0, 1, 5, 0, 1, 0, 5, 1, 0, 1, 0, 1, 5, 0, 1, 0, 1, 5,
    0, 2, 1, 3, 4, 2, 4, 3, 2, 4, 3, 2, 4, 3, 2, 4, 3, 6,
)
FIRST = [sum(WIDTHS[:k]) for k in range(len(WIDTHS))]
LAST = PARTS - 1
PIECES = [(k, n) for k in range(PARTS) for n in range(CUTS[k])]
LATER = [p for p in PIECES if p[1] > 0]
SLOTS = 4

DN_T = (((0,), (0,)), ((), ()))
DN_N = (((1,), (1,)), ((), ()))


def f32dot(a, b, dims=(((1,), (0,)), ((), ()))):
    return lax.dot_general(a, b, dims, preferred_element_type=F32)


def kernel(names, counts, coords_hbm, tiles_hbm, feat_hbm, weight_hbm, gout_hbm, layer_hbm, wgrad, igrad, *refs):
    r = dict(zip(names, refs))
    tiles, adj, feat, weight, gout, layer = (r[n] for n in ("tiles", "adj", "feat", "weight", "gout", "layer"))
    nodes, back, wown, wz, terms_send, terms_recv, table, slot_of = (
        r[n] for n in ("nodes", "back", "wown", "wz", "terms_send", "terms_recv", "table", "slot_of")
    )
    local_sem, out_sem, send_sem, recv_sem = (r[n] for n in ("local_sem", "out_sem", "send_sem", "recv_sem"))
    row = lax.axis_index("row")
    z = lax.axis_index("col")
    f = lax.axis_index("feat")
    y, x = row // SIDE, row % SIDE

    def at(dy, dx, dz):
        return (((y + dy + SIDE) % SIDE) * SIDE + (x + dx + SIDE) % SIDE, (z + dz + DEPTH) % DEPTH, f)

    xp, xm = at(0, 1, 0), at(0, -1, 0)
    yp, ym = at(1, 0, 0), at(-1, 0, 0)
    ways = [xp, xm, yp, ym]
    zpeer = [None] + [at(0, 0, d) for d in range(1, DEPTH)]
    zp, zm = zpeer[1], zpeer[DEPTH - 1]
    other = (row, z, 1 - f)

    def weight_load(k):
        cols = slice(FIRST[k], FIRST[k] + WIDTHS[k])
        return pltpu.make_async_copy(weight_hbm.at[:, cols], weight.at[:, cols], local_sem.at[3 + k])

    coords = r["coords"]
    places = pltpu.make_async_copy(coords_hbm, coords, local_sem.at[4 + PARTS])
    loads = [
        pltpu.make_async_copy(feat_hbm, feat, local_sem.at[0]),
        weight_load(0),
        pltpu.make_async_copy(tiles_hbm, tiles.at[0:TILE], local_sem.at[1]),
        *[weight_load(k) for k in range(1, LAST + 1)],
        pltpu.make_async_copy(gout_hbm, gout, local_sem.at[2]),
    ]
    for load in loads:
        load.start()
    places.start()

    barrier = pltpu.get_barrier_semaphore()
    partners = [xp, xm, yp, ym, other] + zpeer[1:]
    for device in partners:
        pl.semaphore_signal(barrier, inc=1, device_id=device, device_id_type=MESH)

    def send(src, dst, to, slot):
        copy = pltpu.make_async_remote_copy(
            src_ref=src, dst_ref=dst, send_sem=send_sem.at[slot], recv_sem=recv_sem.at[slot],
            device_id=to, device_id_type=MESH,
        )
        copy.start()
        return copy

    def arrive(flight):
        whole, slot = flight
        pltpu.make_async_copy(whole, whole, recv_sem.at[slot]).wait()
        pltpu.make_async_copy(whole, whole, send_sem.at[slot]).wait()

    def find_slots():
        shape = (SIDE**4, TILE)
        slot = lax.broadcasted_iota(jnp.int32, shape, 1)
        place = jnp.broadcast_to(coords[0:1] * SIDE**2 + coords[1:2], shape)
        hit = (place == lax.broadcasted_iota(jnp.int32, shape, 0)) & (slot < counts[0, 0])
        found = jnp.where(hit, slot, TILE)
        table[...] = jnp.min(found.T, axis=0, keepdims=True)
        return pltpu.make_async_copy(table, slot_of, local_sem.at[3 + PARTS])

    def lay_out(first, count):
        def one(n, carry):
            slab = first + n // 2
            tile_row = ((z + slab) % DEPTH) * 2 + n % 2
            start = pl.multiple_of((slab * 2 + n % 2) * TILE, TILE)
            for i in range(SIDE):
                for j in range(SIDE):
                    tile_col = ((y + i) % SIDE) * SIDE + (x + j) % SIDE
                    slot = slot_of[0, tile_row * SIDE * SIDE + tile_col]
                    c = (i * SIDE + j) * TILE
                    adj[pl.ds(start, TILE), c : c + TILE] = tiles[slot]
            return carry

        lax.fori_loop(0, 2 * count, one, 0)

    def scatter_sum(kinds, bufs, slot):
        s1, s2, s3, s4, r1, r2, r3, r4, own = bufs
        first, last = ((2, 3), (0, 1)), ((0, 1), (2, 3))

        def send_all(src, dst, to, phase):
            for n in range(2):
                for d in range(2):
                    send(src.at[n, d], dst.at[n, d], ways[to[n][d]], slot + phase % 2)
            return src, slot + phase % 2

        def each():
            at_q = 0
            for term, q in kinds:
                for n in range(2):

                    def acc(a, t, lo, hi, n=n, term=term, q=q):
                        return term(a, t, lo, hi) if n == 0 else term(t, a, 2 * q + lo, 2 * q + hi)

                    one, two = slice(at_q, at_q + q), slice(2 * at_q, 2 * (at_q + q))
                    yield n, acc, q, one, two, slice(two.start, two.start + q), slice(two.start + q, two.stop)
                at_q += q

        for n, acc, q, one, two, up, down in each():
            for t in range(SIDE):
                s1[n, 0, t, one] = acc(2, t, 0, q).astype(BF16)
                s1[n, 1, t, one] = acc(2, t, q, 2 * q).astype(BF16)
        c = send_all(s1, r1, first, 0)
        yield
        arrive(c)
        for n, acc, q, one, two, up, down in each():
            for t in range(SIDE):
                s2[n, 0, t, up] = (acc(1, t, 0, q) + r1[n, 0, t, one].astype(F32)).astype(BF16)
                s2[n, 0, t, down] = acc(1, t, q, 2 * q).astype(BF16)
                s2[n, 1, t, up] = acc(3, t, 0, q).astype(BF16)
                s2[n, 1, t, down] = (acc(3, t, q, 2 * q) + r1[n, 1, t, one].astype(F32)).astype(BF16)
        c = send_all(s2, r2, first, 1)
        yield
        arrive(c)

        def add(t):
            for n, acc, q, one, two, up, down in each():
                own[n, t, two] = acc(0, t, 0, 2 * q) + r2[n, 0, t, two].astype(F32) + r2[n, 1, t, two].astype(F32)

        add(2)
        for n, acc, q, one, two, up, down in each():
            s3[n, 0, one] = own[n, 2, up].astype(BF16)
            s3[n, 1, one] = own[n, 2, down].astype(BF16)
        c = send_all(s3, r3, last, 2)
        for t in (1, 3, 0):
            add(t)
        yield
        arrive(c)
        for n, acc, q, one, two, up, down in each():
            s4[n, 0, up] = (own[n, 1, up] + r3[n, 0, one].astype(F32)).astype(BF16)
            s4[n, 0, down] = own[n, 1, down].astype(BF16)
            s4[n, 1, up] = own[n, 3, up].astype(BF16)
            s4[n, 1, down] = (own[n, 3, down] + r3[n, 1, one].astype(F32)).astype(BF16)
        c = send_all(s4, r4, last, 3)
        yield
        arrive(c)
        res = [[None, None] for _ in kinds]
        for m, (n, acc, q, one, two, up, down) in enumerate(each()):
            res[m // 2][n] = own[n, 0, two] + r4[n, 0, two].astype(F32) + r4[n, 1, two].astype(F32)
        return res

    def plane_gather(g, slot):
        h, q = TILE // 2, TILE // 4

        def send_all(phase, *moves):
            for src, dst, to in zip(moves[0::2], moves[1::2], (xp, xm, yp, ym)):
                send(src, dst, to, slot + phase % 2)
            whole = (g.at[0, 0:2], g.at[0, 0], g.at[0:2], g.at[0])[phase]
            return whole, slot + phase % 2

        own_h, own_l = g.at[0, 0, 0:h], g.at[0, 0, h:TILE]
        c = send_all(
            0, own_h, g.at[0, 3, 0:h], own_h, g.at[0, 1, 0:h],
            own_l, g.at[3, 0, h:TILE], own_l, g.at[1, 0, h:TILE],
        )
        yield
        arrive(c)
        c = send_all(
            1, g.at[0, 3, 0:q], g.at[0, 2, 0:q], g.at[0, 1, q:h], g.at[0, 2, q:h],
            g.at[3, 0, h : h + q], g.at[2, 0, h : h + q], g.at[1, 0, h + q : TILE], g.at[2, 0, h + q : TILE],
        )
        yield
        arrive(c)
        c = send_all(
            2, g.at[:, 0, h:TILE], g.at[:, 3, h:TILE], g.at[:, 0, h:TILE], g.at[:, 1, h:TILE],
            g.at[0, :, 0:h], g.at[3, :, 0:h], g.at[0, :, 0:h], g.at[1, :, 0:h],
        )
        yield
        arrive(c)
        c = send_all(
            3, g.at[:, 3, h : h + q], g.at[:, 2, h : h + q], g.at[:, 1, h + q : TILE], g.at[:, 2, h + q : TILE],
            g.at[3, :, 0:q], g.at[2, :, 0:q], g.at[1, :, q:h], g.at[2, :, q:h],
        )
        yield
        arrive(c)

    def gather_features():
        mine = nodes.at[f]
        for n in range(2):

            @pl.when(f == n)
            def _():
                nodes[n, 0, 0] = feat[:, n * WIDE : (n + 1) * WIDE]

        yield from plane_gather(mine, SLOTS * PARTS)
        send(mine, nodes.at[f], other, SLOTS * PARTS + 2)
        c = mine, SLOTS * PARTS + 2
        yield
        arrive(c)

    def flow(k):
        hc, slot = WIDTHS[k], SLOTS * k
        cols = slice(FIRST[k], FIRST[k] + hc)
        g, part, pre, delta, bsum, bpart = (r[n + str(k)] for n in ("gath", "part", "pre", "delta", "bsum", "bpart"))
        zsend_p, zsend_m, zrecv_p, zrecv_m = (r[n + str(k)] for n in ("zsend_p", "zsend_m", "zrecv_p", "zrecv_m"))

        if k == 0:
            loads[0].wait()
        loads[1 if k == 0 else 2 + k].wait()
        g[0, 0] = f32dot(feat[...], weight[:, cols]).astype(BF16)
        if k == 0:
            pl.semaphore_wait(barrier, len(partners))
        gather = plane_gather(g, slot)
        next(gather)
        if k == 0:
            places.wait()
            found = find_slots()
            found.start()
            found.wait()
            loads[2].wait()
            tiles[TILE] = jnp.zeros((TILE, TILE), BF16)
            lay_out(3, 3)
        yield
        next(gather)
        if k == 0:
            lay_out(0, 3)
            lay_out(6, 2)
        yield
        yield from gather

        def slabs(first, last):
            value = f32dot(adj[first * SLAB : last * SLAB, :], g[...].reshape(ROWS, hc))
            part[first:last] = value.reshape(last - first, SLAB, hc)

        def send_z(step, up, down):
            send(*up, zp, slot + 2 + step % 2)
            send(*down, zm, slot + 2 + step % 2)
            return (pre.at[0] if step in (3, 7) else pre.at[0:2]), slot + 2 + step % 2

        top, low = slice(0, HALF), slice(HALF, SLAB)
        slabs(3, 6)
        zsend_p[0, top] = part[4, top].astype(BF16)
        zsend_p[0, low] = part[3, low].astype(BF16)
        zsend_m[0, top] = part[5, top].astype(BF16)
        zsend_m[0, low] = part[4, low].astype(BF16)
        c = send_z(0, (zsend_p.at[0], zrecv_p.at[0]), (zsend_m.at[0], zrecv_m.at[0]))
        slabs(6, 8)
        slabs(0, 3)
        yield
        for s in (1, 2):
            arrive(c)
            zsend_p[s, top] = (part[4 - s, top] + zrecv_p[s - 1, top].astype(F32)).astype(BF16)
            zsend_p[s, low] = (part[3 - s, low] + zrecv_p[s - 1, low].astype(F32)).astype(BF16)
            zsend_m[s, top] = (part[5 + s, top] + zrecv_m[s - 1, top].astype(F32)).astype(BF16)
            zsend_m[s, low] = (part[4 + s, low] + zrecv_m[s - 1, low].astype(F32)).astype(BF16)
            c = send_z(s, (zsend_p.at[s], zrecv_p.at[s]), (zsend_m.at[s], zrecv_m.at[s]))
            yield
        arrive(c)
        zsend_p[3, top] = (part[1, top] + zrecv_p[2, top].astype(F32)).astype(BF16)
        zsend_m[3, low] = (part[7, low] + zrecv_m[2, low].astype(F32)).astype(BF16)
        c = send_z(3, (zsend_p.at[3, top], zrecv_p.at[3, top]), (zsend_m.at[3, low], zrecv_m.at[3, low]))
        yield
        arrive(c)
        pre[0, top] = (part[0, top] + zrecv_m[2, top].astype(F32) + zrecv_p[3, top].astype(F32)).astype(BF16)
        pre[0, low] = (part[0, low] + zrecv_p[2, low].astype(F32) + zrecv_m[3, low].astype(F32)).astype(BF16)

        def activate(i):
            start = pl.multiple_of(((z + i) % DEPTH) * SLAB, SLAB)
            value = pre[i].astype(F32)
            sig = 0.5 + 0.5 * jnp.tanh(0.5 * value)
            layer[pl.ds(start, SLAB), cols] = (value * sig).astype(BF16)
            slope = sig * (1.0 + value * (1.0 - sig))
            delta[i * SLAB : (i + 1) * SLAB] = (gout[pl.ds(start, SLAB), cols].astype(F32) * slope).astype(BF16)

        c = send_z(4, (pre.at[0], pre.at[7]), (pre.at[0], pre.at[1]))
        if k == 0:
            loads[-1].wait()
        activate(0)
        yield
        for s in (1, 2):
            arrive(c)
            c = send_z(4 + s, (pre.at[8 - s], pre.at[7 - s]), (pre.at[s], pre.at[s + 1]))
            activate(8 - s)
            activate(s)
            yield
        arrive(c)
        c = send_z(7, (pre.at[5, top], pre.at[4, top]), (pre.at[3, low], pre.at[4, low]))
        activate(5)
        activate(3)
        for n in range(DEPTH):
            c0 = n * SLAB
            bsum[c0 : c0 + SLAB] = f32dot(adj[0 : 4 * SLAB, c0 : c0 + SLAB], delta[0 : 4 * SLAB], DN_T) + f32dot(
                adj[5 * SLAB :, c0 : c0 + SLAB], delta[5 * SLAB :], DN_T
            )
        yield
        arrive(c)
        activate(4)
        mid = slice(4 * SLAB, 5 * SLAB)
        for n in (4, 5, 0, 1, 2, 3, 6, 7):
            c0 = n * SLAB
            value = bsum[c0 : c0 + SLAB] + f32dot(adj[mid, c0 : c0 + SLAB], delta[mid], DN_T)
            bpart[n // 2, n % 2 * 2 : n % 2 * 2 + 2] = value.astype(BF16).reshape(2, TILE, hc)
        out = pltpu.make_async_copy(layer.at[:, cols], layer_hbm.at[:, cols], out_sem.at[k])
        out.start()
        outs.append(out)

    def plane_sums(k, piece):
        hc = WIDTHS[k]
        wide = hc // CUTS[k]
        inner = slice(piece * wide, (piece + 1) * wide)
        cols = slice(FIRST[k] + inner.start, FIRST[k] + inner.stop)
        bpart, wpart = r["bpart" + str(k)], r["wpart" + str(k)]
        if piece == 0:
            block = bpart[...].reshape(ROWS, hc)
            for n in range(2):
                value = f32dot(nodes[n].reshape(ROWS, WIDE), block, DN_T)
                wpart[n * WIDE : (n + 1) * WIDE] = value * ((ROWS * DEPTH) ** -0.5)

        def bterm(i, j, lo, hi):
            return bpart[i, j, lo:hi, inner].astype(F32)

        def wterm(i, j, lo, hi):
            start = (((y + i) % SIDE) * SIDE + (x + j) % SIDE) * (INNER // 16) + lo
            return wpart[pl.ds(pl.multiple_of(start, 16), hi - lo), inner]

        bufs = [r["sum_" + n + str(k) + str(piece)] for n in ("s1", "s2", "s3", "s4", "r1", "r2", "r3", "r4", "own")]
        res = yield from scatter_sum(((bterm, TILE // 4), (wterm, INNER // 64)), bufs, SLOTS * k if piece == 0 else SLOTS * PARTS + 5 + 2 * LATER.index((k, piece)))
        for n in range(2):
            wown[n * 32 : (n + 1) * 32, cols] = res[1][n]
            back[n * TILE // 2 : (n + 1) * TILE // 2, cols] = res[0][n].astype(BF16)

    def finish():
        slot = SLOTS * PARTS + 3
        for d in range(1, DEPTH):
            start = pl.multiple_of(((z + d) % DEPTH) * 8, 8)
            send(wown.at[pl.ds(start, 8)], wz.at[d], zpeer[d], slot)
        theirs = f32dot(back[...], weight[pl.ds(pl.multiple_of((1 - f) * WIDE, WIDE), WIDE)], DN_N)
        terms_send[...] = theirs.astype(BF16)
        send(terms_send, terms_recv, other, slot + 1)
        mine = f32dot(back[...], weight[pl.ds(pl.multiple_of(f * WIDE, WIDE), WIDE)], DN_N)
        total = wown[pl.ds(pl.multiple_of(z * 8, 8), 8)]
        arrive((terms_send, slot + 1))
        igrad[...] = (mine + terms_recv[...].astype(F32)).astype(BF16)
        arrive((wz.at[1:DEPTH], slot))
        for d in range(1, DEPTH):
            total = total + wz[d]
        wgrad[...] = total
        yield

    outs = []
    flows = [flow(k) for k in range(PARTS)] + [plane_sums(k, n) for k, n in PIECES] + [gather_features(), finish()]
    for n in ORDER:
        next(flows[n], None)
    for out in outs:
        out.wait()


def scratch_of():
    dma = pltpu.SemaphoreType.DMA
    slots = SLOTS * PARTS + 5 + 2 * len(LATER)
    refs = {
        "tiles": VMEM((TILE + 1, TILE, TILE), BF16),
        "adj": VMEM((ROWS, ROWS), BF16),
        "feat": VMEM((TILE, INNER), BF16),
        "weight": VMEM((INNER, WIDE), BF16),
        "gout": VMEM((ROWS, WIDE), BF16),
        "layer": VMEM((ROWS, WIDE), BF16),
        "nodes": VMEM((2, SIDE, SIDE, TILE, WIDE), BF16),
        "back": VMEM((TILE, WIDE), BF16),
        "wown": VMEM((INNER // 16, WIDE), F32),
        "wz": VMEM((DEPTH, 8, WIDE), F32),
        "coords": VMEM((2, TILE), jnp.int32),
        "table": VMEM((1, SIDE**4), jnp.int32),
        "slot_of": pltpu.SMEM((1, SIDE**4), jnp.int32),
        "terms_send": VMEM((TILE, WIDE), BF16),
        "terms_recv": VMEM((TILE, WIDE), BF16),
        "local_sem": dma((5 + PARTS,)),
        "out_sem": dma((PARTS,)),
        "send_sem": dma((slots,)),
        "recv_sem": dma((slots,)),
    }
    for k, hc in enumerate(WIDTHS):
        shapes = {
            "gath": ((SIDE, SIDE, TILE, hc), BF16),
            "part": ((DEPTH, SLAB, hc), F32),
            "zsend_p": ((4, SLAB, hc), BF16),
            "zsend_m": ((4, SLAB, hc), BF16),
            "zrecv_p": ((4, SLAB, hc), BF16),
            "zrecv_m": ((4, SLAB, hc), BF16),
            "pre": ((DEPTH, SLAB, hc), BF16),
            "delta": ((ROWS, hc), BF16),
            "bsum": ((ROWS, hc), F32),
            "bpart": ((SIDE, SIDE, TILE, hc), BF16),
            "wpart": ((INNER, hc), F32),
        }
        q, wide = TILE // 4 + INNER // 64, hc // CUTS[k]
        for piece in range(CUTS[k]):
            for way in "sr":
                shapes[f"sum_{way}1{k}{piece}"] = ((2, 2, SIDE, q, wide), BF16)
                shapes[f"sum_{way}2{k}{piece}"] = ((2, 2, SIDE, 2 * q, wide), BF16)
                shapes[f"sum_{way}3{k}{piece}"] = ((2, 2, q, wide), BF16)
                shapes[f"sum_{way}4{k}{piece}"] = ((2, 2, 2 * q, wide), BF16)
            shapes[f"sum_own{k}{piece}"] = ((2, SIDE, 2 * q, wide), F32)
        for name, (shape, dtype) in shapes.items():
            refs[name if name.startswith("sum_") else name + str(k)] = VMEM(shape, dtype)
    return refs


def on_device(tiles, coords, counts, features, weight, grad_out):
    scratch = scratch_of()
    anywhere, hbm = pl.BlockSpec(memory_space=pl.ANY), pl.BlockSpec(memory_space=pltpu.HBM)
    shapes = (
        jax.ShapeDtypeStruct((ROWS, WIDE), BF16),
        jax.ShapeDtypeStruct((8, WIDE), F32),
        jax.ShapeDtypeStruct((TILE, WIDE), BF16),
    )
    large = (coords[0, 0].T, tiles[0, 0], features, weight, grad_out)
    return pl.pallas_call(
        functools.partial(kernel, tuple(scratch)),
        out_shape=shapes,
        in_specs=[pl.BlockSpec(memory_space=pltpu.SMEM)] + [hbm] * 5,
        out_specs=(anywhere, pl.BlockSpec(memory_space=VMEM), pl.BlockSpec(memory_space=VMEM)),
        scratch_shapes=list(scratch.values()),
        compiler_params=pltpu.CompilerParams(
            collective_id=0, has_side_effects=True, vmem_limit_bytes=VMEM_LIMIT
        ),
        cost_estimate=pl.CostEstimate(flops=11 * 10**9, bytes_accessed=10 * 2**20, transcendentals=2**20),
        name="graph_layer",
    )(counts, *[pltpu.with_memory_space_constraint(v, pltpu.HBM) for v in large])

def solution(mesh):
    return jax.shard_map(
        on_device,
        mesh=mesh,
        in_specs=(
            P("row", "col", None, None, None),
            P("row", "col", None, None),
            P("row", "col"),
            P(("col", "row"), None),
            P(None, "feat"),
            P("row", "feat"),
        ),
        out_specs=(P("row", "feat"), P(("row", "col"), "feat"), P(("col", "row"), "feat")),
        check_vma=False,
    )
```
